32 devices in a mesh: loop: 8 (over y, x, core), grp: 4 (over z).
Axes of the slice: x: 2, y: 2, z: 4, core: 2. Of those that a mesh axis runs over, the one named last changes fastest.
Arguments:
- queries: bfloat16 [8192, 512], P(('loop', 'grp')), may hold values from -24 to 24
- key_rows: bfloat16 [8192, 512], P(('loop', 'grp')), may hold values from -4 to 4
- value_rows: bfloat16 [8192, 512], P(('loop', 'grp')), may hold values from -6 to 6
- out_weight: bfloat16 [512, 512], replicated, may hold values from -0.25 to 0.25
- tile_list: int32 [32, 4], P(('loop', 'grp')), may hold values from 0 to 7, as said below
- expander_order: int32 [3, 8192], P(None, ('loop', 'grp')), may hold values from 0 to 255, as said below
- expander_bias: float32 [3, 8], replicated, may hold values from 2 to 6
Outputs:
- layer_output: bfloat16 [8192, 512], P(('loop', 'grp'))
The draws below stay inside these ranges and needn't reach their ends.
Inputs may be any that keep to these rules, and one draw needn't show every extreme that they name: `tile_list`: entry 0 of every row is 3, the partition's own block. Each other entry is 3 + o for a loop offset o with 0 < |o| <= 3, distinct within a row, or the padding value 2 * 3 + 1; every row has at least one non-padding neighbour entry. `expander_order`: for each matching and each partition, the 256 entries of that partition are a permutation of 0 to 255.
All inputs are finite; a program needn't handle non-finite values.
Results may differ from the reference program's by a relative error of at most 0.0075.
Values may be sent and summed in bfloat16 or wider, within the bound.
No kernel may reach another device: no remote copies, remote signals or barrier semaphores. Data moves between devices by JAX's collectives and lax.ppermute only.
A program may use at most 128 MiB of HBM per device.

```python
import math
import jax
import jax.numpy as jnp
from jax import lax

HEADS = 8
HEAD = 64
D = 512
ROWS = 256
RADIUS = 3
TILES = 4
MATCHINGS = 3
PARTS_SIZE = 32
NODES = 8192
N_LOOP = 8
N_GRP = 4


def score_base(key):
    base = jax.random.fold_in(key, 1234)
    shape_all = (NODES, HEADS * HEAD)
    drawn_keys = jnp.clip(jax.random.normal(jax.random.fold_in(base, 1), shape_all, jnp.float32), -4.0, 4.0)
    drawn_queries = jnp.clip(jax.random.normal(jax.random.fold_in(base, 2), shape_all, jnp.float32), -4.0, 4.0)
    return (drawn_keys, drawn_queries)


def draw_key_rows(key, part):
    drawn_keys, drawn_queries = score_base(key)
    return drawn_keys.astype(jnp.bfloat16)


def draw_queries(key, part):
    drawn_keys, drawn_queries = score_base(key)
    return drawn_queries.astype(jnp.bfloat16)


def draw_tile_list(key, part):
    base = jax.random.fold_in(key, 77)
    part_keys = jax.random.split(jax.random.fold_in(base, 1), PARTS_SIZE)
    nonzero = jnp.array([value for value in range(2 * RADIUS + 1) if value != RADIUS], jnp.int32)
    shuffled = jax.vmap(lambda one_key: jax.random.permutation(one_key, nonzero))(part_keys)
    counts = jax.random.randint(jax.random.fold_in(base, 2), (PARTS_SIZE,), 1, TILES)
    counts = counts.at[0].set(TILES - 1).at[1].set(1)
    slot_ids = jnp.arange(TILES - 1, dtype=jnp.int32)[None, :]
    chosen = jnp.where(slot_ids < counts[:, None], shuffled[:, :TILES - 1], 2 * RADIUS + 1)
    chosen = chosen.at[0].set(jnp.array([0, 2 * RADIUS, 1], jnp.int32))
    own_block = jnp.full((PARTS_SIZE, 1), RADIUS, jnp.int32)
    return jnp.concatenate([own_block, chosen], axis=1).astype(jnp.int32)


def draw_expander_order(key, part):
    base = jax.random.fold_in(key, 99)
    row_keys = jax.random.split(base, MATCHINGS * PARTS_SIZE)
    shuffled = jax.vmap(lambda one_key: jax.random.permutation(one_key, ROWS))(row_keys)
    return shuffled.reshape(MATCHINGS, PARTS_SIZE * ROWS).astype(jnp.int32)


def block_levels(rng, shape, cuts, smallest, high):
    factor_of = 1.0
    for dim, shards_of in cuts:
        draws = jax.random.uniform(jax.random.fold_in(jax.random.fold_in(rng, 6), dim), (shards_of,), jnp.float32, smallest / len(cuts), high / len(cuts))
        factor_of = factor_of * jnp.repeat(jnp.exp(draws), shape[dim] // shards_of).reshape((-1,) + (1,) * (len(shape) - 1 - dim))
    return factor_of


def normal_values(rng, shape, spread, bound, cuts=(), kind=jnp.bfloat16):
    gain = block_levels(rng, shape, cuts, -0.22, 0.18) if cuts else 1.0
    drawn = jax.random.normal(rng, shape, jnp.float32) * spread * gain
    return jnp.minimum(jnp.maximum(drawn, -bound), bound).astype(kind)


def setup_inputs(seed: int = 0) -> dict:
    arg_keys = jax.random.split(jax.random.key(seed), 8)
    queries = draw_queries(jax.random.fold_in(arg_keys[7], 71), 0)
    key_rows = draw_key_rows(jax.random.fold_in(arg_keys[7], 71), 0)
    value_rows = normal_values(arg_keys[2], (NODES, D), 1.0, 6.0, ((0, 32),))
    out_weight = normal_values(arg_keys[3], (D, D), D ** -0.5, 0.25)
    tile_list = draw_tile_list(jax.random.fold_in(arg_keys[7], 71), 0)
    expander_order = draw_expander_order(jax.random.fold_in(arg_keys[7], 71), 0)
    expander_bias = jnp.clip(jnp.exp(jax.random.uniform(arg_keys[6], (MATCHINGS, HEADS), jnp.float32, math.log(2.0), math.log(6.0))), 2.0, 6.0)
    return dict(queries=queries, key_rows=key_rows, value_rows=value_rows, out_weight=out_weight, tile_list=tile_list, expander_order=expander_order, expander_bias=expander_bias)


NEG_FILL = -1e30


def partner_nodes(expander_order):
    bucket_size = ROWS // N_GRP
    order_table = expander_order.reshape(MATCHINGS, N_LOOP, N_GRP, ROWS)
    position = jnp.argsort(order_table, axis=-1).astype(jnp.int32)
    bucket_id = position // bucket_size
    partner_pos = jnp.where(bucket_id == 0, jnp.bitwise_xor(position, 1), position)
    group_ids = jnp.arange(N_GRP, dtype=jnp.int32)[None, None, :, None]
    partner_grp = jnp.bitwise_xor(group_ids, bucket_id)
    match_ids = jnp.arange(MATCHINGS, dtype=jnp.int32)[:, None, None, None]
    loop_ids = jnp.arange(N_LOOP, dtype=jnp.int32)[None, :, None, None]
    partner_row = order_table[match_ids, loop_ids, partner_grp, partner_pos]
    partner_ids = (loop_ids * N_GRP + partner_grp) * ROWS + partner_row
    return partner_ids.reshape(MATCHINGS, PARTS_SIZE, ROWS).astype(jnp.int32)


def reference(queries, key_rows, value_rows, out_weight, tile_list, expander_order, expander_bias):
    score_scale = HEAD ** -0.5
    partners = partner_nodes(expander_order)
    query_parts = queries.reshape(PARTS_SIZE, ROWS, HEADS, HEAD)
    key_parts = key_rows.reshape(PARTS_SIZE, ROWS, HEADS, HEAD)
    value_parts = value_rows.reshape(PARTS_SIZE, ROWS, HEADS, HEAD)
    key_nodes = key_rows.reshape(NODES, HEADS, HEAD)
    value_nodes = value_rows.reshape(NODES, HEADS, HEAD)

    def one_part(part_index):
        loop_pos = part_index // N_GRP
        grp_pos = part_index % N_GRP
        tiles_here = tile_list[part_index]
        sources = (((loop_pos + tiles_here - RADIUS) % N_LOOP) * N_GRP + grp_pos).astype(jnp.int32)
        tile_valid = tiles_here <= 2 * RADIUS
        block_keys = key_parts[sources].reshape(TILES * ROWS, HEADS, HEAD).astype(jnp.float32)
        block_vals = value_parts[sources].reshape(TILES * ROWS, HEADS, HEAD).astype(jnp.float32)
        query_here = query_parts[part_index].astype(jnp.float32)
        scores = jnp.einsum("rhe,nhe->hrn", query_here, block_keys) * score_scale
        key_mask = jnp.repeat(tile_valid, ROWS)[None, None, :]
        scores = jnp.where(key_mask, scores, NEG_FILL)
        partner_idx = partners[:, part_index]
        partner_keys = key_nodes[partner_idx].astype(jnp.float32)
        partner_vals = value_nodes[partner_idx].astype(jnp.float32)
        expander_scores = jnp.einsum("rhe,jrhe->jrh", query_here, partner_keys) * score_scale + expander_bias[:, None, :]
        row_max = jnp.maximum(jnp.max(scores, axis=-1).T, jnp.max(expander_scores, axis=0))
        weights = jnp.where(key_mask, jnp.exp(scores - row_max.T[:, :, None]), 0.0)
        expander_w = jnp.exp(expander_scores - row_max[None])
        denominator = jnp.sum(weights, axis=-1).T + jnp.sum(expander_w, axis=0)
        weights_low = lax.optimization_barrier(weights.astype(jnp.bfloat16)).astype(jnp.float32)
        expander_low = lax.optimization_barrier(expander_w.astype(jnp.bfloat16)).astype(jnp.float32)
        numerator = jnp.einsum("hrn,nhe->rhe", weights_low, block_vals)
        numerator = numerator + jnp.sum(expander_low[..., None] * partner_vals, axis=0)
        attended = (numerator / denominator[..., None]).reshape(ROWS, HEADS * HEAD).astype(jnp.bfloat16)
        return jnp.dot(attended, out_weight, preferred_element_type=jnp.float32).astype(jnp.bfloat16)

    outputs = lax.map(one_part, jnp.arange(PARTS_SIZE, dtype=jnp.int32))
    return outputs.reshape(NODES, HEADS * HEAD)
```

```python
import functools

import jax
import jax.numpy as jnp
from jax import lax
from jax.experimental import pallas as pl
from jax.experimental.pallas import tpu as pltpu
from jax.sharding import PartitionSpec as P

HEADS = 8
RADIUS = 3
MATCHINGS = 3
LANES = 128
LOG2E = 1.4426950408889634
NEG_FILL = -1e30
VMEM_BYTES = 40 * 1024 * 1024

F32 = jnp.float32
BF16 = jnp.bfloat16


def dot(a, b, contract=((1,), (0,))):
    return lax.dot_general(a, b, (contract, ((), ())), preferred_element_type=F32)


def place_table(order_row, rows):
    row_ids = lax.broadcasted_iota(jnp.int32, (rows, rows), 0)
    return jnp.where(row_ids == order_row, 1.0, 0.0).astype(BF16)


def prep_kernel(groups, k_ref, v_ref, order_ref, tile_ref, *bucket_refs):
    rows, width = k_ref.shape
    bucket = rows // groups
    half = width // 2
    keys = k_ref[...]
    vals = v_ref[...]
    order = order_ref[...]
    lane = lax.broadcasted_iota(jnp.int32, order.shape, 1)
    swapped = jnp.where(lane % 2 == 0, jnp.roll(order, -1, axis=1), jnp.roll(order, 1, axis=1))
    wanted = jnp.where(lane < bucket, swapped, order)
    for j in range(MATCHINGS):
        table = place_table(wanted[j : j + 1, :], rows)
        ordered_k = dot(table, keys, ((0,), (0,))).astype(BF16)
        ordered_v = dot(table, vals, ((0,), (0,))).astype(BF16)
        for b in range(groups):
            out = slice(j * bucket, (j + 1) * bucket)
            bucket_refs[b][out, :width] = ordered_k[b * bucket : (b + 1) * bucket]
            bucket_refs[b][out, width:] = ordered_v[b * bucket : (b + 1) * bucket]
    tile_ref[:width, :] = vals.T
    tile_ref[width : width + rows, :] = keys[:, :half]
    tile_ref[width + rows :, :] = keys[:, half:]


def blocks_kernel(loop_size, tiles_ref, q_ref, *refs):
    n_bufs = 2 * RADIUS + 1
    bufs = refs[:n_bufs]
    acc_out, stat_out, tile_vmem, qz, acc, m_ref, l_ref, sems = refs[n_bufs:]
    rows, width = q_ref.shape
    head = width // HEADS
    n_tiles = tiles_ref.shape[1]
    here = lax.axis_index("loop")

    def buffer_of(t):
        offset = tiles_ref[0, t]
        if loop_size == 8:
            away = here ^ lax.rem(here + offset - RADIUS + loop_size, loop_size)
            slot = jnp.where(away > 4, away - 1, away)
        else:
            slot = offset
        return slot, offset <= 2 * RADIUS

    for t in range(n_tiles):
        slot, live = buffer_of(t)
        for k in range(n_bufs):

            @pl.when(live & (slot == k))
            def _():
                pltpu.make_async_copy(bufs[k], tile_vmem.at[t], sems.at[t]).start()

    q_t = q_ref[...].T
    zeros = jnp.zeros((head, rows), BF16)
    for h in range(HEADS):
        mine = q_t[h * head : (h + 1) * head]
        parts = (mine, zeros) if h % 2 == 0 else (zeros, mine)
        qz[h] = jnp.concatenate(parts, axis=0)
    m_ref[...] = jnp.full(m_ref.shape, NEG_FILL, F32)
    l_ref[...] = jnp.zeros(l_ref.shape, F32)
    acc[...] = jnp.zeros(acc.shape, F32)
    scale = head ** (-0.5) * LOG2E

    def one_tile(t, carry):
        @pl.when(tiles_ref[0, t] <= 2 * RADIUS)
        def _():
            pltpu.make_async_copy(bufs[0], tile_vmem.at[t], sems.at[t]).wait()
            for h in range(HEADS):
                pair = h // 2
                base = width + (pair // 2) * rows
                keys = tile_vmem[t, base : base + rows, (pair % 2) * LANES : (pair % 2 + 1) * LANES]
                scores = dot(keys, qz[h])
                old = m_ref[h : h + 1, :]
                new = jnp.maximum(old, jnp.max(scores, axis=0, keepdims=True))
                alpha = jnp.exp2((old - new) * scale)
                w = jnp.exp2((scores - new) * scale)
                l_ref[h : h + 1, :] = l_ref[h : h + 1, :] * alpha + jnp.sum(w, axis=0, keepdims=True)
                m_ref[h : h + 1, :] = new
                mine = slice(h * head, (h + 1) * head)
                acc[mine, :] = acc[mine, :] * alpha + dot(tile_vmem[t, mine, :], w.astype(BF16))

        return carry

    lax.fori_loop(0, n_tiles, one_tile, 0)
    acc_out[...] = acc[...].T
    pad = jnp.zeros((LANES - 2 * HEADS, rows), F32)
    stat_out[...] = jnp.concatenate([m_ref[...], l_ref[...], pad], axis=0).T


def finish_kernel(groups, q_ref, order_ref, bias_ref, acc_ref, stat_ref, w_ref, *refs):
    bucket_refs = refs[:groups]
    out_ref = refs[groups]
    rows, width = q_ref.shape
    head = width // HEADS
    bucket = rows // groups
    scale = head ** (-0.5) * LOG2E
    unscale = head**0.5
    gather = (
        lax.broadcasted_iota(jnp.int32, (width, LANES), 0) // head
        == lax.broadcasted_iota(jnp.int32, (width, LANES), 1)
    )
    gather = jnp.where(gather, 1.0, 0.0).astype(BF16)
    spread = (
        lax.broadcasted_iota(jnp.int32, (LANES, width), 1) // head
        == lax.broadcasted_iota(jnp.int32, (LANES, width), 0)
    )
    spread = jnp.where(spread, 1.0, 0.0).astype(BF16)
    queries = q_ref[...].astype(F32)
    stat = stat_ref[...]
    lane = lax.broadcasted_iota(jnp.int32, stat.shape, 1)
    block_max = jnp.where(lane < HEADS, stat, 0.0)
    block_sum = jnp.where(lane < HEADS, jnp.roll(stat, -HEADS, axis=1), 1.0)
    edge_scores = []
    edge_vals = []
    for j in range(MATCHINGS):
        table = place_table(order_ref[j : j + 1, :], rows)
        mine = slice(j * bucket, (j + 1) * bucket)
        in_order = jnp.concatenate([ref[mine, :] for ref in bucket_refs], axis=0)
        partner = dot(table, in_order)
        prod = queries * partner[:, :width]
        high = prod.astype(BF16)
        low = (prod - high.astype(F32)).astype(BF16)
        edge = dot(high, gather) + dot(low, gather)
        edge_scores.append(edge + bias_ref[j : j + 1, :] * unscale)
        edge_vals.append(partner[:, width:])
    top = block_max
    for edge in edge_scores:
        top = jnp.maximum(top, edge)
    keep = jnp.exp2((block_max - top) * scale)
    edge_w = [jnp.exp2((edge - top) * scale) for edge in edge_scores]
    total = block_sum * keep
    for u in edge_w:
        total = total + u
    inv = 1.0 / total

    def wide(x):
        high = x.astype(BF16)
        low = (x - high.astype(F32)).astype(BF16)
        return dot(high, spread) + dot(low, spread)

    numer = acc_ref[...] * wide(keep)
    for u, vals in zip(edge_w, edge_vals):
        numer = numer + dot(u.astype(BF16), spread) * vals
    attended = (numer * wide(inv)).astype(BF16)
    out_ref[...] = dot(attended, w_ref[...]).astype(BF16)


def vmem_specs(n):
    return [pl.BlockSpec(memory_space=pltpu.VMEM)] * n


def shards(groups, loop_size, queries, key_rows, value_rows, out_weight, tile_list, expander_order, expander_bias):
    rows, width = queries.shape
    head = width // HEADS
    bucket = rows // groups
    params = pltpu.CompilerParams(vmem_limit_bytes=VMEM_BYTES)
    tile_shape = jax.ShapeDtypeStruct((width + 2 * rows, width // 2), BF16)
    bucket_shape = jax.ShapeDtypeStruct((MATCHINGS * bucket, 2 * width), BF16)
    own_tile, *outgoing = pl.pallas_call(
        functools.partial(prep_kernel, groups),
        out_shape=[tile_shape] + [bucket_shape] * groups,
        in_specs=vmem_specs(3),
        out_specs=vmem_specs(1 + groups),
        compiler_params=params,
        name="prep",
    )(key_rows, value_rows, expander_order)

    def over_grp(array, b):
        return lax.ppermute(array, "grp", [(i, i ^ b) for i in range(groups)])

    incoming = {b: over_grp(outgoing[b], b) for b in range(groups - 1, 0, -1)}

    def flipped(array, bits):
        return lax.ppermute(array, "loop", [(i, i ^ bits) for i in range(loop_size)])

    if loop_size == 8:
        side = flipped(own_tile, 2)
        across = flipped(own_tile, 5)
        twin = flipped(own_tile, 1)
        corner = flipped(side, 4)
        side_twin = flipped(side, 1)
        corner_twin = flipped(corner, 1)
        tiles = [own_tile, twin, side, side_twin, across, corner, corner_twin]
    else:
        tiles = []
        for offset in range(-RADIUS, RADIUS + 1):
            pairs = [(i, (i - offset) % loop_size) for i in range(loop_size)]
            tiles.append(lax.ppermute(own_tile, "loop", pairs) if offset else own_tile)

    acc, stat = pl.pallas_call(
        functools.partial(blocks_kernel, loop_size),
        out_shape=[
            jax.ShapeDtypeStruct((rows, width), F32),
            jax.ShapeDtypeStruct((rows, LANES), F32),
        ],
        in_specs=[pl.BlockSpec(memory_space=pltpu.SMEM)]
        + vmem_specs(1)
        + [pl.BlockSpec(memory_space=pl.ANY)] * len(tiles),
        out_specs=vmem_specs(2),
        scratch_shapes=[
            pltpu.VMEM((tile_list.shape[1],) + tile_shape.shape, BF16),
            pltpu.VMEM((HEADS, 2 * head, rows), BF16),
            pltpu.VMEM((width, rows), F32),
            pltpu.VMEM((HEADS, rows), F32),
            pltpu.VMEM((HEADS, rows), F32),
            pltpu.SemaphoreType.DMA((tile_list.shape[1],)),
        ],
        compiler_params=params,
        name="blocks",
    )(tile_list, queries, *tiles)

    bias = jnp.pad(expander_bias, ((0, 0), (0, LANES - HEADS)))
    buckets = [outgoing[0]] + [incoming[b] for b in range(1, groups)]
    return pl.pallas_call(
        functools.partial(finish_kernel, groups),
        out_shape=jax.ShapeDtypeStruct((rows, width), BF16),
        in_specs=vmem_specs(6 + groups),
        out_specs=pl.BlockSpec(memory_space=pltpu.VMEM),
        compiler_params=params,
        name="finish",
    )(queries, expander_order, bias, acc, stat, out_weight, *buckets)


def solution(mesh):
    placed = (
        P(("loop", "grp"), None),
        P(("loop", "grp"), None),
        P(("loop", "grp"), None),
        P(),
        P(("loop", "grp"), None),
        P(None, ("loop", "grp")),
        P(),
    )
    return jax.shard_map(
        functools.partial(shards, mesh.shape["grp"], mesh.shape["loop"]),
        mesh=mesh,
        in_specs=placed,
        out_specs=P(("loop", "grp"), None),
        check_vma=False,
    )
```

```python
import functools

import jax
import jax.numpy as jnp
from jax import lax
from jax.experimental import pallas as pl
from jax.experimental.pallas import tpu as pltpu
from jax.sharding import PartitionSpec as P

HEADS = 8
RADIUS = 3
MATCHINGS = 3
LANES = 128
LOG2E = 1.4426950408889634
NEG_FILL = -1e30
VMEM_BYTES = 40 * 1024 * 1024

F32 = jnp.float32
BF16 = jnp.bfloat16


def dot(a, b, contract=((1,), (0,))):
    return lax.dot_general(a, b, (contract, ((), ())), preferred_element_type=F32)


def place_table(order_row, rows):
    row_ids = lax.broadcasted_iota(jnp.int32, (rows, rows), 0)
    return jnp.where(row_ids == order_row, 1.0, 0.0).astype(BF16)


def prep_kernel(groups, k_hbm, v_hbm, order_hbm, tile_ref, out_ref, k_ref, v_ref, order_ref, sems):
    rows, width = k_ref.shape
    bucket = rows // groups
    half = width // 2
    group = lax.axis_index("grp")
    copies = [
        pltpu.make_async_copy(src, dst, sems.at[i])
        for i, (src, dst) in enumerate(((order_hbm, order_ref), (k_hbm, k_ref), (v_hbm, v_ref)))
    ]
    for copy in copies:
        copy.start()
    for copy in copies:
        copy.wait()
    keys = k_ref[...]
    vals = v_ref[...]
    order = order_ref[...]
    lane = lax.broadcasted_iota(jnp.int32, order.shape, 1)
    swapped = jnp.where(lane % 2 == 0, jnp.roll(order, -1, axis=1), jnp.roll(order, 1, axis=1))
    wanted = jnp.where(lane < bucket, swapped, order)
    for j in range(MATCHINGS):
        table = place_table(wanted[j : j + 1, :], rows)
        ordered_k = dot(table, keys, ((0,), (0,))).astype(BF16)
        ordered_v = dot(table, vals, ((0,), (0,))).astype(BF16)
        for b in range(groups):
            mine = slice(j * bucket, (j + 1) * bucket)
            out_ref[group ^ b, mine, :width] = ordered_k[b * bucket : (b + 1) * bucket]
            out_ref[group ^ b, mine, width:] = ordered_v[b * bucket : (b + 1) * bucket]
    tile_ref[:width, :] = vals.T
    tile_ref[width : width + rows, :] = keys[:, :half]
    tile_ref[width + rows :, :] = keys[:, half:]


def blocks_kernel(loop_size, served, first, last, tiles_ref, q_ref, *refs):
    n_bufs = 2 * RADIUS + 1
    rows, width = q_ref.shape
    head = width // HEADS
    n_tiles = tiles_ref.shape[1]
    refs = list(refs)
    bufs = {}
    for slot, split in served.items():
        if split:
            bufs[slot] = (refs.pop(0), refs.pop(0))
        else:
            whole = refs.pop(0)
            bufs[slot] = (whole.at[:width, :], whole.at[width:, :])
    state = () if first else (refs.pop(0), refs.pop(0))
    acc_out, stat_out = refs.pop(0), refs.pop(0)
    tile_vmem, qz, acc, m_ref, l_ref, sems = refs
    here = lax.axis_index("loop")

    def slot_of(t):
        offset = tiles_ref[0, t]
        slot = offset
        if loop_size == 8:
            away = here ^ lax.rem(here + offset - RADIUS + loop_size, loop_size)
            slot = jnp.where(away > 4, away - 1, away)
        return jnp.where(offset <= 2 * RADIUS, slot, n_bufs)

    def here_served(slot):
        return functools.reduce(jnp.logical_or, [slot == k for k in served])

    def halves(slot, t):
        vals, keys = bufs[slot]
        return (
            pltpu.make_async_copy(vals, tile_vmem.at[t, :width, :], sems.at[t, 0]),
            pltpu.make_async_copy(keys, tile_vmem.at[t, width:, :], sems.at[t, 1]),
        )

    for t in range(n_tiles):
        slot = slot_of(t)
        for k in served:

            @pl.when(slot == k)
            def _():
                for copy in halves(k, t):
                    copy.start()

    q_t = q_ref[...].T
    zeros = jnp.zeros((head, rows), BF16)
    for h in range(HEADS):
        mine = q_t[h * head : (h + 1) * head]
        parts = (mine, zeros) if h % 2 == 0 else (zeros, mine)
        qz[h] = jnp.concatenate(parts, axis=0)
    if first:
        m_ref[...] = jnp.full(m_ref.shape, NEG_FILL, F32)
        l_ref[...] = jnp.zeros(l_ref.shape, F32)
        acc[...] = jnp.zeros(acc.shape, F32)
    else:
        acc[...] = state[0][...]
        m_ref[...] = state[1][:HEADS]
        l_ref[...] = state[1][HEADS:]
    scale = head ** (-0.5) * LOG2E

    def one_tile(t, carry):
        @pl.when(here_served(slot_of(t)))
        def _():
            for copy in halves(next(iter(served)), t):
                copy.wait()
            for h in range(HEADS):
                pair = h // 2
                base = width + (pair // 2) * rows
                keys = tile_vmem[t, base : base + rows, (pair % 2) * LANES : (pair % 2 + 1) * LANES]
                scores = dot(keys, qz[h])
                old = m_ref[h : h + 1, :]
                new = jnp.maximum(old, jnp.max(scores, axis=0, keepdims=True))
                alpha = jnp.exp2((old - new) * scale)
                w = jnp.exp2((scores - new) * scale)
                l_ref[h : h + 1, :] = l_ref[h : h + 1, :] * alpha + jnp.sum(w, axis=0, keepdims=True)
                m_ref[h : h + 1, :] = new
                mine = slice(h * head, (h + 1) * head)
                acc[mine, :] = acc[mine, :] * alpha + dot(tile_vmem[t, mine, :], w.astype(BF16))

        return carry

    lax.fori_loop(0, n_tiles, one_tile, 0)
    if last:
        acc_out[...] = acc[...].T
        pad = jnp.zeros((LANES - 2 * HEADS, rows), F32)
        stat_out[...] = jnp.concatenate([m_ref[...], l_ref[...], pad], axis=0).T
    else:
        acc_out[...] = acc[...]
        stat_out[:HEADS] = m_ref[...]
        stat_out[HEADS:] = l_ref[...]


def finish_kernel(groups, q_ref, order_ref, bias_ref, acc_ref, stat_ref, w_ref, come_ref, out_ref):
    group = lax.axis_index("grp")
    rows, width = q_ref.shape
    head = width // HEADS
    bucket = rows // groups
    scale = head ** (-0.5) * LOG2E
    unscale = head**0.5
    gather = (
        lax.broadcasted_iota(jnp.int32, (width, LANES), 0) // head
        == lax.broadcasted_iota(jnp.int32, (width, LANES), 1)
    )
    gather = jnp.where(gather, 1.0, 0.0).astype(BF16)
    spread = (
        lax.broadcasted_iota(jnp.int32, (LANES, width), 1) // head
        == lax.broadcasted_iota(jnp.int32, (LANES, width), 0)
    )
    spread = jnp.where(spread, 1.0, 0.0).astype(BF16)
    queries = q_ref[...].astype(F32)
    stat = stat_ref[...]
    lane = lax.broadcasted_iota(jnp.int32, stat.shape, 1)
    block_max = jnp.where(lane < HEADS, stat, 0.0)
    block_sum = jnp.where(lane < HEADS, jnp.roll(stat, -HEADS, axis=1), 1.0)
    edge_scores = []
    edge_vals = []
    for j in range(MATCHINGS):
        table = place_table(order_ref[j : j + 1, :], rows)
        mine = slice(j * bucket, (j + 1) * bucket)
        come = [come_ref[group ^ b, mine, :] for b in range(1, groups)]
        in_order = jnp.concatenate([come_ref[group, mine, :]] + come, axis=0)
        partner = dot(table, in_order)
        prod = queries * partner[:, :width]
        high = prod.astype(BF16)
        low = (prod - high.astype(F32)).astype(BF16)
        edge = dot(high, gather) + dot(low, gather)
        edge_scores.append(edge + bias_ref[j : j + 1, :] * unscale)
        edge_vals.append(partner[:, width:])
    top = block_max
    for edge in edge_scores:
        top = jnp.maximum(top, edge)
    keep = jnp.exp2((block_max - top) * scale)
    edge_w = [jnp.exp2((edge - top) * scale) for edge in edge_scores]
    total = block_sum * keep
    for u in edge_w:
        total = total + u
    inv = 1.0 / total

    def wide(x):
        high = x.astype(BF16)
        low = (x - high.astype(F32)).astype(BF16)
        return dot(high, spread) + dot(low, spread)

    numer = acc_ref[...] * wide(keep)
    for u, vals in zip(edge_w, edge_vals):
        numer = numer + dot(u.astype(BF16), spread) * vals
    attended = (numer * wide(inv)).astype(BF16)
    out_ref[...] = dot(attended, w_ref[...]).astype(BF16)


def vmem_specs(n):
    return [pl.BlockSpec(memory_space=pltpu.VMEM)] * n


def shards(groups, loop_size, queries, key_rows, value_rows, out_weight, tile_list, expander_order, expander_bias):
    rows, width = queries.shape
    head = width // HEADS
    bucket = rows // groups
    params = pltpu.CompilerParams(vmem_limit_bytes=VMEM_BYTES)
    tile_shape = jax.ShapeDtypeStruct((width + 2 * rows, width // 2), BF16)
    bucket_shape = jax.ShapeDtypeStruct((groups, MATCHINGS * bucket, 2 * width), BF16)
    own_tile, outgoing = pl.pallas_call(
        functools.partial(prep_kernel, groups),
        out_shape=[tile_shape, bucket_shape],
        in_specs=[pl.BlockSpec(memory_space=pltpu.HBM)] * 3,
        out_specs=vmem_specs(2),
        scratch_shapes=[
            pltpu.VMEM((rows, width), BF16),
            pltpu.VMEM((rows, width), BF16),
            pltpu.VMEM(expander_order.shape, jnp.int32),
            pltpu.SemaphoreType.DMA((3,)),
        ],
        compiler_params=params,
        name="prep",
    )(key_rows, value_rows, expander_order)

    incoming = lax.all_to_all(outgoing, "grp", split_axis=0, concat_axis=0, tiled=True)

    def flipped(array, bits):
        return lax.ppermute(array, "loop", [(i, i ^ bits) for i in range(loop_size)])

    def attend(served, state, last):
        slots = {slot: len(arrays) == 2 for slot, arrays in served.items()}
        arrays = [array for group in served.values() for array in group]
        if last:
            acc_shape, stat_shape = (rows, width), (rows, LANES)
        else:
            acc_shape, stat_shape = (width, rows), (2 * HEADS, rows)
        return pl.pallas_call(
            functools.partial(blocks_kernel, loop_size, slots, not state, last),
            out_shape=[jax.ShapeDtypeStruct(acc_shape, F32), jax.ShapeDtypeStruct(stat_shape, F32)],
            in_specs=[pl.BlockSpec(memory_space=pltpu.SMEM)]
            + vmem_specs(1)
            + [pl.BlockSpec(memory_space=pl.ANY)] * len(arrays)
            + vmem_specs(len(state)),
            out_specs=vmem_specs(2),
            scratch_shapes=[
                pltpu.VMEM((tile_list.shape[1],) + tile_shape.shape, BF16),
                pltpu.VMEM((HEADS, 2 * head, rows), BF16),
                pltpu.VMEM((width, rows), F32),
                pltpu.VMEM((HEADS, rows), F32),
                pltpu.VMEM((HEADS, rows), F32),
                pltpu.SemaphoreType.DMA((tile_list.shape[1], 2)),
            ],
            compiler_params=params,
            name="corner_blocks" if state else "blocks",
        )(tile_list, queries, *arrays, *state)

    if loop_size == 8:
        side = flipped(own_tile, 2)
        across = flipped(own_tile, 5)
        twin = flipped(own_tile, 1)
        side, across = lax.optimization_barrier((side, across))
        corner_k = flipped(side[width:], 4)
        corner_v = flipped(across[:width], 3)
        side_twin = flipped(side, 1)
        corner_twin_k = flipped(corner_k, 1)
        corner_twin_v = flipped(corner_v, 1)
        state = attend({0: [own_tile], 1: [twin], 2: [side], 3: [side_twin], 4: [across]}, (), False)
        corners = {5: [corner_v, corner_k], 6: [corner_twin_v, corner_twin_k]}
        acc, stat = attend(corners, state, True)
    else:
        tiles = {}
        for offset in range(-RADIUS, RADIUS + 1):
            pairs = [(i, (i - offset) % loop_size) for i in range(loop_size)]
            tile = lax.ppermute(own_tile, "loop", pairs) if offset else own_tile
            tiles[offset + RADIUS] = [tile]
        acc, stat = attend(tiles, (), True)

    bias = jnp.pad(expander_bias, ((0, 0), (0, LANES - HEADS)))
    return pl.pallas_call(
        functools.partial(finish_kernel, groups),
        out_shape=jax.ShapeDtypeStruct((rows, width), BF16),
        in_specs=vmem_specs(7),
        out_specs=pl.BlockSpec(memory_space=pltpu.VMEM),
        compiler_params=params,
        name="finish",
    )(queries, expander_order, bias, acc, stat, out_weight, incoming)


def solution(mesh):
    placed = (
        P(("loop", "grp"), None),
        P(("loop", "grp"), None),
        P(("loop", "grp"), None),
        P(),
        P(("loop", "grp"), None),
        P(None, ("loop", "grp")),
        P(),
    )
    return jax.shard_map(
        functools.partial(shards, mesh.shape["grp"], mesh.shape["loop"]),
        mesh=mesh,
        in_specs=placed,
        out_specs=P(("loop", "grp"), None),
        check_vma=False,
    )
```

```python
import functools

import jax
import jax.numpy as jnp
from jax import lax
from jax.experimental import pallas as pl
from jax.experimental.pallas import tpu as pltpu
from jax.sharding import PartitionSpec as P

HEADS = 8
RADIUS = 3
MATCHINGS = 3
LANES = 128
ORDER_ROWS = 16
LOG2E = 1.4426950408889634
NEG_FILL = -1e30
VMEM_BYTES = 40 * 1024 * 1024

CHEAP = pl.CostEstimate(flops=1000, bytes_accessed=1000, transcendentals=0)
LONG = pl.CostEstimate(flops=2 * 10**9, bytes_accessed=1000, transcendentals=0)
F32 = jnp.float32
BF16 = jnp.bfloat16


def dot(a, b, contract=((1,), (0,))):
    return lax.dot_general(a, b, (contract, ((), ())), preferred_element_type=F32)


def place_table(order_row, rows):
    row_ids = lax.broadcasted_iota(jnp.int32, (rows, rows), 0)
    return jnp.where(row_ids == order_row, 1.0, 0.0).astype(BF16)


def prep_kernel(groups, k_hbm, v_hbm, order_hbm, tile_ref, *refs):
    out_refs = refs[:groups]
    k_ref, v_ref, order_ref, sems = refs[groups:]
    rows, width = k_ref.shape
    bucket = rows // groups
    half = width // 2
    copies = [
        pltpu.make_async_copy(src, dst, sems.at[i])
        for i, (src, dst) in enumerate(((order_hbm, order_ref), (v_hbm, v_ref), (k_hbm, k_ref)))
    ]
    for copy in copies:
        copy.start()
    for copy in copies:
        copy.wait()
    keys = k_ref[...]
    vals = v_ref[...]
    order = order_ref[...]
    tile_ref[:width, :] = vals.T
    tile_ref[width : width + rows, :] = keys[:, :half]
    tile_ref[width + rows :, :] = keys[:, half:]
    for ref in out_refs:
        if ref.shape[0] > MATCHINGS * bucket:
            ref[:rows, :] = keys
            below = slice(rows, rows + ORDER_ROWS)
            padded = jnp.concatenate([order, jnp.zeros((ORDER_ROWS - MATCHINGS, rows), jnp.int32)], axis=0)
            ref[below, :rows] = padded.astype(F32).astype(BF16)
            ref[below, rows:] = jnp.zeros((ORDER_ROWS, width - rows), BF16)
    lane = lax.broadcasted_iota(jnp.int32, order.shape, 1)
    swapped = jnp.where(lane % 2 == 0, jnp.roll(order, -1, axis=1), jnp.roll(order, 1, axis=1))
    wanted = jnp.where(lane < bucket, swapped, order)
    n_paired = sum(ref.shape[1] == 2 * width for ref in out_refs)
    for j in range(MATCHINGS):
        table = place_table(wanted[j : j + 1, :], rows)
        ordered_k = dot(table[:, : n_paired * bucket], keys, ((0,), (0,))).astype(BF16)
        ordered_v = dot(table, vals, ((0,), (0,))).astype(BF16)
        for b, out_ref in enumerate(out_refs):
            first = out_ref.shape[0] - MATCHINGS * bucket + j * bucket
            mine = slice(first, first + bucket)
            at = slice(b * bucket, (b + 1) * bucket)
            if b < n_paired:
                out_ref[mine, :width] = ordered_k[at]
                out_ref[mine, width:] = ordered_v[at]
            else:
                out_ref[mine, :] = ordered_v[at]


def relay_kernel(groups, message_ref, mine_ref, next_ref):
    bucket = mine_ref.shape[0] // MATCHINGS
    rows = bucket * groups
    keys = message_ref[:rows, :]
    order = message_ref[rows : rows + ORDER_ROWS, :rows].astype(F32).astype(jnp.int32)
    for j in range(MATCHINGS):
        table = place_table(order[j : j + 1, :], rows)[:, 2 * bucket :]
        ordered = dot(table, keys, ((0,), (0,))).astype(BF16)
        mine = slice(j * bucket, (j + 1) * bucket)
        mine_ref[mine, :] = ordered[:bucket]
        next_ref[mine, :] = ordered[bucket:]


def blocks_kernel(loop_size, served, first, last, tiles_ref, q_ref, *refs):
    n_bufs = 2 * RADIUS + 1
    rows, width = q_ref.shape
    head = width // HEADS
    n_tiles = tiles_ref.shape[1]
    refs = list(refs)
    bufs = {}
    for slot, split in served.items():
        if split:
            bufs[slot] = (refs.pop(0), refs.pop(0))
        else:
            whole = refs.pop(0)
            bufs[slot] = (whole.at[:width, :], whole.at[width:, :])
    state = () if first else (refs.pop(0), refs.pop(0))
    acc_out, stat_out = refs.pop(0), refs.pop(0)
    tile_vmem, qz, acc, m_ref, l_ref, sems = refs
    here = lax.axis_index("loop")

    def slot_of(t):
        offset = tiles_ref[0, t]
        slot = offset
        if loop_size == 8:
            away = here ^ lax.rem(here + offset - RADIUS + loop_size, loop_size)
            slot = jnp.where(away > 4, away - 1, away)
        return jnp.where(offset <= 2 * RADIUS, slot, n_bufs)

    def here_served(slot):
        return functools.reduce(jnp.logical_or, [slot == k for k in served])

    def halves(slot, t):
        vals, keys = bufs[slot]
        return (
            pltpu.make_async_copy(vals, tile_vmem.at[t, :width, :], sems.at[t, 0]),
            pltpu.make_async_copy(keys, tile_vmem.at[t, width:, :], sems.at[t, 1]),
        )

    for t in range(n_tiles):
        slot = slot_of(t)
        for k in served:

            @pl.when(slot == k)
            def _():
                for copy in halves(k, t):
                    copy.start()

    q_t = q_ref[...].T
    zeros = jnp.zeros((head, rows), BF16)
    for h in range(HEADS):
        mine = q_t[h * head : (h + 1) * head]
        parts = (mine, zeros) if h % 2 == 0 else (zeros, mine)
        qz[h] = jnp.concatenate(parts, axis=0)
    if first:
        m_ref[...] = jnp.full(m_ref.shape, NEG_FILL, F32)
        l_ref[...] = jnp.zeros(l_ref.shape, F32)
        acc[...] = jnp.zeros(acc.shape, F32)
    else:
        acc[...] = state[0][...]
        m_ref[...] = state[1][:HEADS]
        l_ref[...] = state[1][HEADS:]
    scale = head ** (-0.5) * LOG2E

    def one_tile(t, carry):
        @pl.when(here_served(slot_of(t)))
        def _():
            for copy in halves(next(iter(served)), t):
                copy.wait()
            for h in range(HEADS):
                pair = h // 2
                base = width + (pair // 2) * rows
                keys = tile_vmem[t, base : base + rows, (pair % 2) * LANES : (pair % 2 + 1) * LANES]
                scores = dot(keys, qz[h])
                old = m_ref[h : h + 1, :]
                new = jnp.maximum(old, jnp.max(scores, axis=0, keepdims=True))
                alpha = jnp.exp2((old - new) * scale)
                w = jnp.exp2((scores - new) * scale)
                l_ref[h : h + 1, :] = l_ref[h : h + 1, :] * alpha + jnp.sum(w, axis=0, keepdims=True)
                m_ref[h : h + 1, :] = new
                mine = slice(h * head, (h + 1) * head)
                acc[mine, :] = acc[mine, :] * alpha + dot(tile_vmem[t, mine, :], w.astype(BF16))

        return carry

    lax.fori_loop(0, n_tiles, one_tile, 0)
    if last:
        acc_out[...] = acc[...].T
        pad = jnp.zeros((LANES - 2 * HEADS, rows), F32)
        stat_out[...] = jnp.concatenate([m_ref[...], l_ref[...], pad], axis=0).T
    else:
        acc_out[...] = acc[...]
        stat_out[:HEADS] = m_ref[...]
        stat_out[HEADS:] = l_ref[...]


def rows_in_order(refs, j, bucket, first, width):
    parts = []
    for ref in refs:
        top = ref.shape[0] - (MATCHINGS - j) * bucket
        left = first if ref.shape[1] == 2 * width else 0
        parts.append(ref[top : top + bucket, left : left + width])
    return jnp.concatenate(parts, axis=0)


def weigh_kernel(groups, q_ref, order_ref, bias_ref, acc_ref, stat_ref, *refs):
    key_refs = refs[:groups]
    val_refs = refs[groups : 2 * groups - 1]
    part_ref, edge_ref = refs[2 * groups - 1 :]
    rows, width = q_ref.shape
    head = width // HEADS
    bucket = rows // groups
    scale = head ** (-0.5) * LOG2E
    unscale = head**0.5
    gather = (
        lax.broadcasted_iota(jnp.int32, (width, LANES), 0) // head
        == lax.broadcasted_iota(jnp.int32, (width, LANES), 1)
    )
    gather = jnp.where(gather, 1.0, 0.0).astype(BF16)
    spread = (
        lax.broadcasted_iota(jnp.int32, (LANES, width), 1) // head
        == lax.broadcasted_iota(jnp.int32, (LANES, width), 0)
    )
    spread = jnp.where(spread, 1.0, 0.0).astype(BF16)
    queries = q_ref[...].astype(F32)
    stat = stat_ref[...]
    lane = lax.broadcasted_iota(jnp.int32, stat.shape, 1)
    block_max = jnp.where(lane < HEADS, stat, 0.0)
    block_sum = jnp.where(lane < HEADS, jnp.roll(stat, -HEADS, axis=1), 1.0)
    edge_scores = []
    for j in range(MATCHINGS):
        table = place_table(order_ref[j : j + 1, :], rows)
        prod = queries * dot(table, rows_in_order(key_refs, j, bucket, 0, width))
        high = prod.astype(BF16)
        low = (prod - high.astype(F32)).astype(BF16)
        edge = dot(high, gather) + dot(low, gather)
        edge_scores.append(edge + bias_ref[j : j + 1, :] * unscale)
    top = block_max
    for edge in edge_scores:
        top = jnp.maximum(top, edge)
    keep = jnp.exp2((block_max - top) * scale)
    edge_w = [jnp.exp2((edge - top) * scale) for edge in edge_scores]
    total = block_sum * keep
    for u in edge_w:
        total = total + u
    inv = 1.0 / total

    def wide(x):
        high = x.astype(BF16)
        low = (x - high.astype(F32)).astype(BF16)
        return dot(high, spread) + dot(low, spread)

    numer = acc_ref[...] * wide(keep * inv)
    for j in range(MATCHINGS):
        table = place_table(order_ref[j : j + 1, :], rows)[:, : rows - bucket]
        edge = wide(edge_w[j].astype(BF16).astype(F32) * inv)
        edge_ref[j] = edge
        numer = numer + edge * dot(table, rows_in_order(val_refs, j, bucket, width, width))
    part_ref[...] = numer


def finish_kernel(groups, order_ref, part_ref, edge_ref, w_ref, val_ref, out_ref):
    rows, width = part_ref.shape
    bucket = rows // groups
    numer = part_ref[...]
    for j in range(MATCHINGS):
        table = place_table(order_ref[j : j + 1, :], rows)[:, rows - bucket :]
        numer = numer + edge_ref[j] * dot(table, rows_in_order([val_ref], j, bucket, width, width))
    out_ref[...] = dot(numer.astype(BF16), w_ref[...]).astype(BF16)


fence = lax.optimization_barrier


def vmem_specs(n):
    return [pl.BlockSpec(memory_space=pltpu.VMEM)] * n


def shards(groups, loop_size, queries, key_rows, value_rows, out_weight, tile_list, expander_order, expander_bias):
    rows, width = queries.shape
    head = width // HEADS
    bucket = rows // groups
    params = pltpu.CompilerParams(vmem_limit_bytes=VMEM_BYTES)
    tile_shape = jax.ShapeDtypeStruct((width + 2 * rows, width // 2), BF16)
    relayed = loop_size == 8 and groups == 4
    kv_shape = jax.ShapeDtypeStruct((MATCHINGS * bucket, 2 * width), BF16)
    one_shape = jax.ShapeDtypeStruct((MATCHINGS * bucket, width), BF16)
    message_shape = jax.ShapeDtypeStruct((rows + ORDER_ROWS + MATCHINGS * bucket, width), BF16)
    bucket_shapes = [kv_shape, kv_shape, message_shape, one_shape] if relayed else [kv_shape] * groups
    own_tile, *outgoing = pl.pallas_call(
        functools.partial(prep_kernel, groups),
        out_shape=[tile_shape] + bucket_shapes,
        in_specs=[pl.BlockSpec(memory_space=pltpu.HBM)] * 3,
        out_specs=vmem_specs(1 + groups),
        scratch_shapes=[
            pltpu.VMEM((rows, width), BF16),
            pltpu.VMEM((rows, width), BF16),
            pltpu.VMEM(expander_order.shape, jnp.int32),
            pltpu.SemaphoreType.DMA((3,)),
        ],
        name="prep",
    )(key_rows, value_rows, expander_order)

    def over_grp(array, b):
        return lax.ppermute(array, "grp", [(i, i ^ b) for i in range(groups)])

    def flipped(array, bits):
        return lax.ppermute(array, "loop", [(i, i ^ bits) for i in range(loop_size)])

    def attend(served, state, last):
        slots = {slot: len(arrays) == 2 for slot, arrays in served.items()}
        arrays = [array for group in served.values() for array in group]
        if last:
            acc_shape, stat_shape = (rows, width), (rows, LANES)
        else:
            acc_shape, stat_shape = (width, rows), (2 * HEADS, rows)
        return pl.pallas_call(
            functools.partial(blocks_kernel, loop_size, slots, not state, last),
            out_shape=[jax.ShapeDtypeStruct(acc_shape, F32), jax.ShapeDtypeStruct(stat_shape, F32)],
            in_specs=[pl.BlockSpec(memory_space=pltpu.SMEM)]
            + vmem_specs(1)
            + [pl.BlockSpec(memory_space=pl.ANY)] * len(arrays)
            + vmem_specs(len(state)),
            out_specs=vmem_specs(2),
            scratch_shapes=[
                pltpu.VMEM((tile_list.shape[1],) + tile_shape.shape, BF16),
                pltpu.VMEM((HEADS, 2 * head, rows), BF16),
                pltpu.VMEM((width, rows), F32),
                pltpu.VMEM((HEADS, rows), F32),
                pltpu.VMEM((HEADS, rows), F32),
                pltpu.SemaphoreType.DMA((tile_list.shape[1], 2)),
            ],
            compiler_params=params,
            cost_estimate=CHEAP,
            name="blocks" + "_".join(map(str, served)),
        )(tile_list, queries, *arrays, *state)

    if relayed:
        message = over_grp(outgoing[2], 2)
        near = over_grp(outgoing[1], 1)
        side = flipped(own_tile, 2)
        across = flipped(own_tile, 5)
        state = attend({0: [own_tile]}, (), False)
        side, across, tile, state = fence((side, across, own_tile, state))
        twin = flipped(tile, 1)
        corner_k = flipped(side[width:], 4)
        corner_v = flipped(across[:width], 3)
        state = attend({2: [side], 4: [across]}, state, False)
        message, near, state = fence((message, near, state))
        keys_2, passed = pl.pallas_call(
            functools.partial(relay_kernel, groups),
            out_shape=[one_shape] * 2,
            in_specs=vmem_specs(1),
            out_specs=vmem_specs(2),
            compiler_params=params,
            cost_estimate=LONG,
            name="relay",
        )(message)
        corner_k, corner_v, twin, side, keys_2, passed, far_vals, state = fence(
            (corner_k, corner_v, twin, side, keys_2, passed, outgoing[3], state)
        )
        side_twin = flipped(side, 1)
        corner_twin_k = flipped(corner_k, 1)
        corner_twin_v = flipped(corner_v, 1)
        keys_3 = over_grp(passed, 1)
        vals_3 = over_grp(far_vals, 3)
        late = {1: [twin], 3: [side_twin], 5: [corner_v, corner_k], 6: [corner_twin_v, corner_twin_k]}
        acc, stat = attend(late, state, True)
        key_parts = [outgoing[0], near, keys_2, keys_3]
        val_parts = [outgoing[0], near, message, vals_3]
    else:
        tiles = {}
        for offset in range(-RADIUS, RADIUS + 1):
            pairs = [(i, (i - offset) % loop_size) for i in range(loop_size)]
            tile = lax.ppermute(own_tile, "loop", pairs) if offset else own_tile
            tiles[offset + RADIUS] = [tile]
        acc, stat = attend(tiles, (), True)
        key_parts = val_parts = [outgoing[0]] + [over_grp(outgoing[b], b) for b in range(1, groups)]

    bias = jnp.pad(expander_bias, ((0, 0), (0, LANES - HEADS)))
    part, edge = pl.pallas_call(
        functools.partial(weigh_kernel, groups),
        out_shape=[
            jax.ShapeDtypeStruct((rows, width), F32),
            jax.ShapeDtypeStruct((MATCHINGS, rows, width), F32),
        ],
        in_specs=vmem_specs(4 + 2 * groups),
        out_specs=vmem_specs(2),
        compiler_params=params,
        cost_estimate=CHEAP,
        name="weigh",
    )(queries, expander_order, bias, acc, stat, *key_parts, *val_parts[:-1])
    return pl.pallas_call(
        functools.partial(finish_kernel, groups),
        out_shape=jax.ShapeDtypeStruct((rows, width), BF16),
        in_specs=vmem_specs(5),
        out_specs=pl.BlockSpec(memory_space=pltpu.VMEM),
        compiler_params=params,
        cost_estimate=CHEAP,
        name="finish",
    )(expander_order, part, edge, out_weight, val_parts[-1])


def solution(mesh):
    placed = (
        P(("loop", "grp"), None),
        P(("loop", "grp"), None),
        P(("loop", "grp"), None),
        P(),
        P(("loop", "grp"), None),
        P(None, ("loop", "grp")),
        P(),
    )
    return jax.shard_map(
        functools.partial(shards, mesh.shape["grp"], mesh.shape["loop"]),
        mesh=mesh,
        in_specs=placed,
        out_specs=P(("loop", "grp"), None),
        check_vma=False,
    )
```

```python
import functools

import jax
import jax.numpy as jnp
from jax import lax
from jax.experimental import pallas as pl
from jax.experimental.pallas import tpu as pltpu
from jax.sharding import PartitionSpec as P

HEADS = 8
RADIUS = 3
MATCHINGS = 3
LANES = 128
ORDER_ROWS = 16
LOG2E = 1.4426950408889634
NEG_FILL = -1e30
VMEM_BYTES = 40 * 1024 * 1024

CHEAP = pl.CostEstimate(flops=1000, bytes_accessed=1000, transcendentals=0)
F32 = jnp.float32
BF16 = jnp.bfloat16


def dot(a, b, contract=((1,), (0,))):
    return lax.dot_general(a, b, (contract, ((), ())), preferred_element_type=F32)


def place_table(order_row, rows):
    row_ids = lax.broadcasted_iota(jnp.int32, (rows, rows), 0)
    return jnp.where(row_ids == order_row, 1.0, 0.0).astype(BF16)


def prep_kernel(groups, k_hbm, v_hbm, order_hbm, tile_ref, *refs):
    out_refs = refs[:-4]
    k_ref, v_ref, order_ref, sems = refs[-4:]
    rows, width = k_ref.shape
    bucket = rows // groups
    half = width // 2
    copies = [
        pltpu.make_async_copy(src, dst, sems.at[i])
        for i, (src, dst) in enumerate(((order_hbm, order_ref), (v_hbm, v_ref), (k_hbm, k_ref)))
    ]
    for copy in copies:
        copy.start()
    for copy in copies:
        copy.wait()
    keys = k_ref[...]
    vals = v_ref[...]
    order = order_ref[...]
    tile_ref[:width, :] = vals.T
    tile_ref[width : width + rows, :] = keys[:, :half]
    tile_ref[width + rows :, :] = keys[:, half:]
    paired = [ref for ref in out_refs if ref.shape[1] == 2 * width]
    for ref in out_refs[len(paired) :]:
        ref[:rows, :] = keys
        padded = jnp.concatenate([order, jnp.zeros((ORDER_ROWS - MATCHINGS, rows), jnp.int32)], axis=0)
        ref[rows:, :rows] = padded.astype(F32).astype(BF16)
        ref[rows:, rows:] = jnp.zeros((ORDER_ROWS, width - rows), BF16)
    lane = lax.broadcasted_iota(jnp.int32, order.shape, 1)
    swapped = jnp.where(lane % 2 == 0, jnp.roll(order, -1, axis=1), jnp.roll(order, 1, axis=1))
    wanted = jnp.where(lane < bucket, swapped, order)
    for j in range(MATCHINGS):
        table = place_table(wanted[j : j + 1, :], rows)[:, : len(paired) * bucket]
        ordered_k = dot(table, keys, ((0,), (0,))).astype(BF16)
        ordered_v = dot(table, vals, ((0,), (0,))).astype(BF16)
        mine = slice(j * bucket, (j + 1) * bucket)
        for b, out_ref in enumerate(paired):
            at = slice(b * bucket, (b + 1) * bucket)
            out_ref[mine, :width] = ordered_k[at]
            out_ref[mine, width:] = ordered_v[at]


def relay_kernel(groups, order_ref, rows_ref, mine_ref, next_ref):
    bucket = mine_ref.shape[0] // MATCHINGS
    rows = bucket * groups
    full = rows_ref[:rows, :]
    order = order_ref[rows:, :rows].astype(F32).astype(jnp.int32)
    for j in range(MATCHINGS):
        table = place_table(order[j : j + 1, :], rows)[:, 2 * bucket :]
        ordered = dot(table, full, ((0,), (0,))).astype(BF16)
        mine = slice(j * bucket, (j + 1) * bucket)
        mine_ref[mine, :] = ordered[:bucket]
        next_ref[mine, :] = ordered[bucket:]


def blocks_kernel(loop_size, served, first, last, tiles_ref, *refs):
    n_bufs = 2 * RADIUS + 1
    refs = list(refs)
    bufs = {slot: refs.pop(0) for slot in served}
    if first:
        q_ref, pairs_ref = refs.pop(0), None
    else:
        pairs_ref, acc_in, stat_in = refs.pop(0), refs.pop(0), refs.pop(0)
    acc_out, stat_out = refs.pop(0), refs.pop(0)
    if pairs_ref is None:
        pairs_ref = refs.pop(0)
    if last:
        acc, stat, tile_vmem, sems = refs
    else:
        (acc, stat), (tile_vmem, sems) = (acc_out, stat_out), refs
    width, rows = acc.shape
    head = width // HEADS
    n_tiles = tiles_ref.shape[1]
    here = lax.axis_index("loop")

    def slot_of(t):
        offset = tiles_ref[0, t]
        slot = offset
        if loop_size == 8:
            away = here ^ lax.rem(here + offset - RADIUS + loop_size, loop_size)
            slot = jnp.where(away > 4, away - 1, away)
        return jnp.where(offset <= 2 * RADIUS, slot, n_bufs)

    def here_served(slot):
        return functools.reduce(jnp.logical_or, [slot == k for k in served])

    def fetch(slot, t):
        return pltpu.make_async_copy(bufs[slot], tile_vmem.at[t], sems.at[t])

    for t in range(n_tiles):
        slot = slot_of(t)
        for k in served:

            @pl.when(slot == k)
            def _():
                fetch(k, t).start()

    if first:
        q_t = q_ref[...].T
        zeros = jnp.zeros((head, rows), BF16)
        for p in range(HEADS // 2):
            even = q_t[2 * p * head : (2 * p + 1) * head]
            odd = q_t[(2 * p + 1) * head : (2 * p + 2) * head]
            pairs_ref[p, :head, :rows] = even
            pairs_ref[p, :head, rows:] = zeros
            pairs_ref[p, head:, :rows] = zeros
            pairs_ref[p, head:, rows:] = odd
        stat[:HEADS] = jnp.full((HEADS, rows), NEG_FILL, F32)
        stat[HEADS:] = jnp.zeros((HEADS, rows), F32)
        acc[...] = jnp.zeros(acc.shape, F32)
    else:
        acc[...] = acc_in[...]
        stat[...] = stat_in[...]
    scale = head ** (-0.5) * LOG2E

    def one_tile(t, carry):
        @pl.when(here_served(slot_of(t)))
        def _():
            fetch(next(iter(served)), t).wait()
            scores = []
            for p in range(HEADS // 2):
                base = width + (p // 2) * rows
                keys = tile_vmem[t, base : base + rows, (p % 2) * LANES : (p % 2 + 1) * LANES]
                scores.append(dot(keys, pairs_ref[p]))
            for p in range(HEADS // 2):
                old = jnp.concatenate([stat[2 * p : 2 * p + 1], stat[2 * p + 1 : 2 * p + 2]], axis=1)
                new = jnp.maximum(old, jnp.max(scores[p], axis=0, keepdims=True))
                alpha = jnp.exp2((old - new) * scale)
                w = jnp.exp2((scores[p] - new) * scale)
                total = jnp.sum(w, axis=0, keepdims=True)
                w = w.astype(BF16)
                for side in range(2):
                    h = 2 * p + side
                    half = slice(side * rows, (side + 1) * rows)
                    mine = slice(h * head, (h + 1) * head)
                    stat[h : h + 1] = new[:, half]
                    stat[HEADS + h : HEADS + h + 1] = stat[HEADS + h : HEADS + h + 1] * alpha[:, half] + total[:, half]
                    acc[mine, :] = acc[mine, :] * alpha[:, half] + dot(tile_vmem[t, mine, :], w[:, half])

        return carry

    lax.fori_loop(0, n_tiles, one_tile, 0)
    if last:
        acc_out[...] = acc[...].T
        pad = jnp.zeros((LANES - 2 * HEADS, rows), F32)
        stat_out[...] = jnp.concatenate([stat[...], pad], axis=0).T


def rows_in_order(refs, j, bucket, first, width):
    parts = []
    for ref in refs:
        top = ref.shape[0] - (MATCHINGS - j) * bucket
        left = first if ref.shape[1] == 2 * width else 0
        parts.append(ref[top : top + bucket, left : left + width])
    return jnp.concatenate(parts, axis=0)


def weigh_kernel(groups, q_ref, order_ref, bias_ref, acc_ref, stat_ref, *refs):
    key_refs = refs[:groups]
    val_refs = refs[groups : 2 * groups - 1]
    part_ref, edge_ref = refs[2 * groups - 1 :]
    rows, width = q_ref.shape
    head = width // HEADS
    bucket = rows // groups
    scale = head ** (-0.5) * LOG2E
    unscale = head**0.5
    gather = (
        lax.broadcasted_iota(jnp.int32, (width, LANES), 0) // head
        == lax.broadcasted_iota(jnp.int32, (width, LANES), 1)
    )
    gather = jnp.where(gather, 1.0, 0.0).astype(BF16)
    spread = (
        lax.broadcasted_iota(jnp.int32, (LANES, width), 1) // head
        == lax.broadcasted_iota(jnp.int32, (LANES, width), 0)
    )
    spread = jnp.where(spread, 1.0, 0.0).astype(BF16)
    queries = q_ref[...].astype(F32)
    stat = stat_ref[...]
    lane = lax.broadcasted_iota(jnp.int32, stat.shape, 1)
    block_max = jnp.where(lane < HEADS, stat, 0.0)
    block_sum = jnp.where(lane < HEADS, jnp.roll(stat, -HEADS, axis=1), 1.0)
    edge_scores = []
    for j in range(MATCHINGS):
        table = place_table(order_ref[j : j + 1, :], rows)
        prod = queries * dot(table, rows_in_order(key_refs, j, bucket, 0, width))
        high = prod.astype(BF16)
        low = (prod - high.astype(F32)).astype(BF16)
        edge = dot(high, gather) + dot(low, gather)
        edge_scores.append(edge + bias_ref[j : j + 1, :] * unscale)
    top = block_max
    for edge in edge_scores:
        top = jnp.maximum(top, edge)
    keep = jnp.exp2((block_max - top) * scale)
    edge_w = [jnp.exp2((edge - top) * scale) for edge in edge_scores]
    total = block_sum * keep
    for u in edge_w:
        total = total + u
    inv = 1.0 / total

    def wide(x):
        high = x.astype(BF16)
        low = (x - high.astype(F32)).astype(BF16)
        return dot(high, spread) + dot(low, spread)

    numer = acc_ref[...] * wide(keep * inv)
    for j in range(MATCHINGS):
        table = place_table(order_ref[j : j + 1, :], rows)[:, : rows - bucket]
        edge = wide(edge_w[j].astype(BF16).astype(F32) * inv)
        edge_ref[j] = edge
        numer = numer + edge * dot(table, rows_in_order(val_refs, j, bucket, width, width))
    part_ref[...] = numer


def finish_kernel(groups, order_ref, part_ref, edge_ref, w_ref, val_ref, out_ref):
    rows, width = part_ref.shape
    bucket = rows // groups
    numer = part_ref[...]
    for j in range(MATCHINGS):
        table = place_table(order_ref[j : j + 1, :], rows)[:, rows - bucket :]
        numer = numer + edge_ref[j] * dot(table, rows_in_order([val_ref], j, bucket, width, width))
    out_ref[...] = dot(numer.astype(BF16), w_ref[...]).astype(BF16)


fence = lax.optimization_barrier


def vmem_specs(n):
    return [pl.BlockSpec(memory_space=pltpu.VMEM)] * n


def shards(groups, loop_size, queries, key_rows, value_rows, out_weight, tile_list, expander_order, expander_bias):
    rows, width = queries.shape
    head = width // HEADS
    bucket = rows // groups
    params = pltpu.CompilerParams(vmem_limit_bytes=VMEM_BYTES)
    tile_shape = jax.ShapeDtypeStruct((width + 2 * rows, width // 2), BF16)
    relayed = loop_size == 8 and groups == 4
    kv_shape = jax.ShapeDtypeStruct((MATCHINGS * bucket, 2 * width), BF16)
    one_shape = jax.ShapeDtypeStruct((MATCHINGS * bucket, width), BF16)
    full_shape = jax.ShapeDtypeStruct((rows + ORDER_ROWS, width), BF16)
    bucket_shapes = [kv_shape, kv_shape, full_shape] if relayed else [kv_shape] * groups
    own_tile, *outgoing = pl.pallas_call(
        functools.partial(prep_kernel, groups),
        out_shape=[tile_shape] + bucket_shapes,
        in_specs=[pl.BlockSpec(memory_space=pltpu.HBM)] * 3,
        out_specs=vmem_specs(1 + len(bucket_shapes)),
        scratch_shapes=[
            pltpu.VMEM((rows, width), BF16),
            pltpu.VMEM((rows, width), BF16),
            pltpu.VMEM(expander_order.shape, jnp.int32),
            pltpu.SemaphoreType.DMA((3,)),
        ],
        name="prep",
    )(key_rows, value_rows, expander_order)

    def over_grp(array, b):
        return lax.ppermute(array, "grp", [(i, i ^ b) for i in range(groups)])

    def flipped(array, bits):
        return lax.ppermute(array, "loop", [(i, i ^ bits) for i in range(loop_size)])

    def attend(served, state, last):
        shapes = [(width, rows), (2 * HEADS, rows)]
        if last:
            shapes = [(rows, width), (rows, LANES)] + shapes
        out_shape = [jax.ShapeDtypeStruct(shape, F32) for shape in shapes[:2]]
        scratch = [pltpu.VMEM(shape, F32) for shape in shapes[2:]]
        pairs_shape = jax.ShapeDtypeStruct((HEADS // 2, 2 * head, 2 * rows), BF16)
        if state is None:
            out_shape.append(pairs_shape)
        others = [queries] if state is None else state
        aliases = {} if state is None or last else {len(served) + 2: 0, len(served) + 3: 1}
        acc, stat, *pairs = pl.pallas_call(
            functools.partial(blocks_kernel, loop_size, tuple(served), state is None, last),
            out_shape=out_shape,
            in_specs=[pl.BlockSpec(memory_space=pltpu.SMEM)]
            + [pl.BlockSpec(memory_space=pl.ANY)] * len(served)
            + vmem_specs(len(others)),
            out_specs=vmem_specs(len(out_shape)),
            scratch_shapes=scratch
            + [
                pltpu.VMEM((tile_list.shape[1],) + tile_shape.shape, BF16),
                pltpu.SemaphoreType.DMA((tile_list.shape[1],)),
            ],
            input_output_aliases=aliases,
            compiler_params=params,
            cost_estimate=CHEAP,
            name="blocks" + "_".join(map(str, served)),
        )(tile_list, *served.values(), *others)
        return [pairs[0] if state is None else state[0], acc, stat]

    if relayed:

        def relay(order, full, name):
            return pl.pallas_call(
                functools.partial(relay_kernel, groups),
                out_shape=[one_shape] * 2,
                in_specs=vmem_specs(2),
                out_specs=vmem_specs(2),
                compiler_params=params,
                cost_estimate=CHEAP,
                name=name,
            )(order, full)

        full_k = over_grp(outgoing[2], 2)
        near = over_grp(outgoing[1], 1)
        side = flipped(own_tile, 2)
        across = flipped(own_tile, 5)
        twin = flipped(own_tile, 1)
        state = attend({0: own_tile}, None, False)
        side, across, twin, own_vals, state = fence((side, across, twin, value_rows, state))
        corner = flipped(side, 4)
        corner_twin = flipped(across, 2)
        side_twin = flipped(side, 1)
        full_v = over_grp(own_vals, 2)
        keys_2, passed = relay(full_k, full_k, "relay_keys")
        keys_3 = over_grp(passed, 1)
        state = attend({1: twin, 2: side, 4: across}, state, False)
        full_v, near, keys_3, state = fence((full_v, near, keys_3, state))
        vals_2, passed = relay(full_k, full_v, "relay_vals")
        vals_3 = over_grp(passed, 1)
        key_parts = [outgoing[0], near, keys_2, keys_3]
        val_parts = [outgoing[0], near, vals_2, vals_3]
        late = {3: side_twin, 5: corner, 6: corner_twin}
        _, acc, stat = attend(late, state, True)
    else:
        tiles = {}
        for offset in range(-RADIUS, RADIUS + 1):
            pairs = [(i, (i - offset) % loop_size) for i in range(loop_size)]
            tile = lax.ppermute(own_tile, "loop", pairs) if offset else own_tile
            tiles[offset + RADIUS] = tile
        _, acc, stat = attend(tiles, None, True)
        key_parts = val_parts = [outgoing[0]] + [over_grp(outgoing[b], b) for b in range(1, groups)]

    bias = jnp.pad(expander_bias, ((0, 0), (0, LANES - HEADS)))
    part, edge = pl.pallas_call(
        functools.partial(weigh_kernel, groups),
        out_shape=[
            jax.ShapeDtypeStruct((rows, width), F32),
            jax.ShapeDtypeStruct((MATCHINGS, rows, width), F32),
        ],
        in_specs=vmem_specs(4 + 2 * groups),
        out_specs=vmem_specs(2),
        compiler_params=params,
        cost_estimate=CHEAP,
        name="weigh",
    )(queries, expander_order, bias, acc, stat, *key_parts, *val_parts[:-1])
    return pl.pallas_call(
        functools.partial(finish_kernel, groups),
        out_shape=jax.ShapeDtypeStruct((rows, width), BF16),
        in_specs=vmem_specs(5),
        out_specs=pl.BlockSpec(memory_space=pltpu.VMEM),
        compiler_params=params,
        cost_estimate=CHEAP,
        name="finish",
    )(expander_order, part, edge, out_weight, val_parts[-1])


def solution(mesh):
    placed = (
        P(("loop", "grp"), None),
        P(("loop", "grp"), None),
        P(("loop", "grp"), None),
        P(),
        P(("loop", "grp"), None),
        P(None, ("loop", "grp")),
        P(),
    )
    return jax.shard_map(
        functools.partial(shards, mesh.shape["grp"], mesh.shape["loop"]),
        mesh=mesh,
        in_specs=placed,
        out_specs=P(("loop", "grp"), None),
        check_vma=False,
    )
```

```python
import functools

import jax
import jax.numpy as jnp
from jax import lax
from jax.experimental import pallas as pl
from jax.experimental.pallas import tpu as pltpu
from jax.sharding import PartitionSpec as P

HEADS = 8
RADIUS = 3
MATCHINGS = 3
LANES = 128
ORDER_ROWS = 16
LOG2E = 1.4426950408889634
NEG_FILL = -1e30
VMEM_BYTES = 40 * 1024 * 1024

LONG = pl.CostEstimate(flops=10**10, bytes_accessed=1000, transcendentals=0)
CHEAP = pl.CostEstimate(flops=1000, bytes_accessed=1000, transcendentals=0)
F32 = jnp.float32
BF16 = jnp.bfloat16


def dot(a, b, contract=((1,), (0,))):
    return lax.dot_general(a, b, (contract, ((), ())), preferred_element_type=F32)


def place_table(order_row, rows):
    row_ids = lax.broadcasted_iota(jnp.int32, (rows, rows), 0)
    return jnp.where(row_ids == order_row, 1.0, 0.0).astype(BF16)


def prep_kernel(groups, k_hbm, v_hbm, order_hbm, tile_ref, *refs):
    out_refs = refs[:-4]
    k_ref, v_ref, order_ref, sems = refs[-4:]
    rows, width = k_ref.shape
    bucket = rows // groups
    half = width // 2
    copies = [
        pltpu.make_async_copy(src, dst, sems.at[i])
        for i, (src, dst) in enumerate(((order_hbm, order_ref), (v_hbm, v_ref), (k_hbm, k_ref)))
    ]
    for copy in copies:
        copy.start()
    for copy in copies:
        copy.wait()
    keys = k_ref[...]
    vals = v_ref[...]
    order = order_ref[...]
    tile_ref[:width, :] = vals.T
    tile_ref[width : width + rows, :] = keys[:, :half]
    tile_ref[width + rows :, :] = keys[:, half:]
    paired = [ref for ref in out_refs if ref.shape[1] == 2 * width]
    for ref in out_refs[len(paired) :]:
        ref[:rows, :] = keys
        padded = jnp.concatenate([order, jnp.zeros((ORDER_ROWS - MATCHINGS, rows), jnp.int32)], axis=0)
        ref[rows:, :rows] = padded.astype(F32).astype(BF16)
        ref[rows:, rows:] = jnp.zeros((ORDER_ROWS, width - rows), BF16)
    lane = lax.broadcasted_iota(jnp.int32, order.shape, 1)
    swapped = jnp.where(lane % 2 == 0, jnp.roll(order, -1, axis=1), jnp.roll(order, 1, axis=1))
    wanted = jnp.where(lane < bucket, swapped, order)
    for j in range(MATCHINGS):
        table = place_table(wanted[j : j + 1, :], rows)[:, : len(paired) * bucket]
        ordered_k = dot(table, keys, ((0,), (0,))).astype(BF16)
        ordered_v = dot(table, vals, ((0,), (0,))).astype(BF16)
        mine = slice(j * bucket, (j + 1) * bucket)
        for b, out_ref in enumerate(paired):
            at = slice(b * bucket, (b + 1) * bucket)
            out_ref[mine, :width] = ordered_k[at]
            out_ref[mine, width:] = ordered_v[at]


def relay_kernel(groups, order_ref, rows_ref, mine_ref, next_ref):
    bucket = mine_ref.shape[0] // MATCHINGS
    rows = bucket * groups
    full = rows_ref[:rows, :]
    order = order_ref[rows:, :rows].astype(F32).astype(jnp.int32)
    for j in range(MATCHINGS):
        table = place_table(order[j : j + 1, :], rows)[:, 2 * bucket :]
        ordered = dot(table, full, ((0,), (0,))).astype(BF16)
        mine = slice(j * bucket, (j + 1) * bucket)
        mine_ref[mine, :] = ordered[:bucket]
        next_ref[mine, :] = ordered[bucket:]


def blocks_kernel(loop_size, served, first, last, tiles_ref, *refs):
    n_bufs = 2 * RADIUS + 1
    refs = list(refs)
    bufs = {slot: refs.pop(0) for slot in served}
    if first:
        q_ref, pairs_ref = refs.pop(0), None
    else:
        pairs_ref, acc_in, stat_in = refs.pop(0), refs.pop(0), refs.pop(0)
    acc_out, stat_out = refs.pop(0), refs.pop(0)
    if pairs_ref is None:
        pairs_ref = refs.pop(0)
    if last:
        acc, stat, tile_vmem, sems = refs
    else:
        (acc, stat), (tile_vmem, sems) = (acc_out, stat_out), refs
    width, rows = acc.shape
    head = width // HEADS
    n_tiles = tiles_ref.shape[1]
    here = lax.axis_index("loop")

    def slot_of(t):
        offset = tiles_ref[0, t]
        slot = offset
        if loop_size == 8:
            away = here ^ lax.rem(here + offset - RADIUS + loop_size, loop_size)
            slot = jnp.where(away > 4, away - 1, away)
        return jnp.where(offset <= 2 * RADIUS, slot, n_bufs)

    def here_served(slot):
        return functools.reduce(jnp.logical_or, [slot == k for k in served])

    def fetch(slot, t):
        return pltpu.make_async_copy(bufs[slot], tile_vmem.at[t], sems.at[t])

    for t in range(n_tiles):
        slot = slot_of(t)
        for k in served:

            @pl.when(slot == k)
            def _():
                fetch(k, t).start()

    if first:
        q_t = q_ref[...].T
        zeros = jnp.zeros((head, rows), BF16)
        for p in range(HEADS // 2):
            even = q_t[2 * p * head : (2 * p + 1) * head]
            odd = q_t[(2 * p + 1) * head : (2 * p + 2) * head]
            pairs_ref[p, :head, :rows] = even
            pairs_ref[p, :head, rows:] = zeros
            pairs_ref[p, head:, :rows] = zeros
            pairs_ref[p, head:, rows:] = odd
        stat[:HEADS] = jnp.full((HEADS, rows), NEG_FILL, F32)
        stat[HEADS:] = jnp.zeros((HEADS, rows), F32)
        acc[...] = jnp.zeros(acc.shape, F32)
    else:
        acc[...] = acc_in[...]
        stat[...] = stat_in[...]
    scale = head ** (-0.5) * LOG2E

    def one_tile(t, carry):
        @pl.when(here_served(slot_of(t)))
        def _():
            fetch(next(iter(served)), t).wait()
            scores = []
            for p in range(HEADS // 2):
                base = width + (p // 2) * rows
                keys = tile_vmem[t, base : base + rows, (p % 2) * LANES : (p % 2 + 1) * LANES]
                scores.append(dot(keys, pairs_ref[p]))
            for p in range(HEADS // 2):
                old = jnp.concatenate([stat[2 * p : 2 * p + 1], stat[2 * p + 1 : 2 * p + 2]], axis=1)
                new = jnp.maximum(old, jnp.max(scores[p], axis=0, keepdims=True))
                alpha = jnp.exp2((old - new) * scale)
                w = jnp.exp2((scores[p] - new) * scale)
                total = jnp.sum(w, axis=0, keepdims=True)
                w = w.astype(BF16)
                for side in range(2):
                    h = 2 * p + side
                    half = slice(side * rows, (side + 1) * rows)
                    mine = slice(h * head, (h + 1) * head)
                    stat[h : h + 1] = new[:, half]
                    stat[HEADS + h : HEADS + h + 1] = stat[HEADS + h : HEADS + h + 1] * alpha[:, half] + total[:, half]
                    acc[mine, :] = acc[mine, :] * alpha[:, half] + dot(tile_vmem[t, mine, :], w[:, half])

        return carry

    lax.fori_loop(0, n_tiles, one_tile, 0)
    if last:
        acc_out[...] = acc[...].T
        pad = jnp.zeros((LANES - 2 * HEADS, rows), F32)
        stat_out[...] = jnp.concatenate([stat[...], pad], axis=0).T


def rows_in_order(refs, j, bucket, first, width):
    parts = []
    for ref in refs:
        top = ref.shape[0] - (MATCHINGS - j) * bucket
        left = first if ref.shape[1] == 2 * width else 0
        parts.append(ref[top : top + bucket, left : left + width])
    return jnp.concatenate(parts, axis=0)


def weigh_kernel(groups, q_ref, order_ref, bias_ref, acc_ref, stat_ref, *refs):
    key_refs = refs[:groups]
    val_refs = refs[groups : 2 * groups - 1]
    part_ref, edge_ref = refs[2 * groups - 1 :]
    rows, width = q_ref.shape
    head = width // HEADS
    bucket = rows // groups
    scale = head ** (-0.5) * LOG2E
    unscale = head**0.5
    gather = (
        lax.broadcasted_iota(jnp.int32, (width, LANES), 0) // head
        == lax.broadcasted_iota(jnp.int32, (width, LANES), 1)
    )
    gather = jnp.where(gather, 1.0, 0.0).astype(BF16)
    spread = (
        lax.broadcasted_iota(jnp.int32, (LANES, width), 1) // head
        == lax.broadcasted_iota(jnp.int32, (LANES, width), 0)
    )
    spread = jnp.where(spread, 1.0, 0.0).astype(BF16)
    queries = q_ref[...].astype(F32)
    stat = stat_ref[...]
    lane = lax.broadcasted_iota(jnp.int32, stat.shape, 1)
    block_max = jnp.where(lane < HEADS, stat, 0.0)
    block_sum = jnp.where(lane < HEADS, jnp.roll(stat, -HEADS, axis=1), 1.0)
    edge_scores = []
    for j in range(MATCHINGS):
        table = place_table(order_ref[j : j + 1, :], rows)
        prod = queries * dot(table, rows_in_order(key_refs, j, bucket, 0, width))
        high = prod.astype(BF16)
        low = (prod - high.astype(F32)).astype(BF16)
        edge = dot(high, gather) + dot(low, gather)
        edge_scores.append(edge + bias_ref[j : j + 1, :] * unscale)
    top = block_max
    for edge in edge_scores:
        top = jnp.maximum(top, edge)
    keep = jnp.exp2((block_max - top) * scale)
    edge_w = [jnp.exp2((edge - top) * scale) for edge in edge_scores]
    total = block_sum * keep
    for u in edge_w:
        total = total + u
    inv = 1.0 / total

    def wide(x):
        high = x.astype(BF16)
        low = (x - high.astype(F32)).astype(BF16)
        return dot(high, spread) + dot(low, spread)

    numer = acc_ref[...] * wide(keep * inv)
    for j in range(MATCHINGS):
        table = place_table(order_ref[j : j + 1, :], rows)[:, : rows - bucket]
        edge = wide(edge_w[j].astype(BF16).astype(F32) * inv)
        edge_ref[j] = edge
        numer = numer + edge * dot(table, rows_in_order(val_refs, j, bucket, width, width))
    part_ref[...] = numer


def finish_kernel(groups, val_ref, order_ref, part_ref, edge_ref, w_ref, out_ref):
    rows, width = part_ref.shape
    bucket = rows // groups
    numer = part_ref[...]
    for j in range(MATCHINGS):
        table = place_table(order_ref[j : j + 1, :], rows)[:, rows - bucket :]
        numer = numer + edge_ref[j] * dot(table, rows_in_order([val_ref], j, bucket, width, width))
    out_ref[...] = dot(numer.astype(BF16), w_ref[...]).astype(BF16)


fence = lax.optimization_barrier


def vmem_specs(n):
    return [pl.BlockSpec(memory_space=pltpu.VMEM)] * n


def shards(groups, loop_size, queries, key_rows, value_rows, out_weight, tile_list, expander_order, expander_bias):
    rows, width = queries.shape
    head = width // HEADS
    bucket = rows // groups
    params = pltpu.CompilerParams(vmem_limit_bytes=VMEM_BYTES)
    tile_shape = jax.ShapeDtypeStruct((width + 2 * rows, width // 2), BF16)
    relayed = loop_size == 8 and groups == 4
    kv_shape = jax.ShapeDtypeStruct((MATCHINGS * bucket, 2 * width), BF16)
    one_shape = jax.ShapeDtypeStruct((MATCHINGS * bucket, width), BF16)
    full_shape = jax.ShapeDtypeStruct((rows + ORDER_ROWS, width), BF16)
    bucket_shapes = [kv_shape, kv_shape, full_shape] if relayed else [kv_shape] * groups
    own_tile, *outgoing = pl.pallas_call(
        functools.partial(prep_kernel, groups),
        out_shape=[tile_shape] + bucket_shapes,
        in_specs=[pl.BlockSpec(memory_space=pltpu.HBM)] * 3,
        out_specs=vmem_specs(1 + len(bucket_shapes)),
        scratch_shapes=[
            pltpu.VMEM((rows, width), BF16),
            pltpu.VMEM((rows, width), BF16),
            pltpu.VMEM(expander_order.shape, jnp.int32),
            pltpu.SemaphoreType.DMA((3,)),
        ],
        name="prep",
    )(key_rows, value_rows, expander_order)

    def over_grp(array, b):
        return lax.ppermute(array, "grp", [(i, i ^ b) for i in range(groups)])

    def flipped(array, bits):
        return lax.ppermute(array, "loop", [(i, i ^ bits) for i in range(loop_size)])

    def attend(served, state, last):
        shapes = [(width, rows), (2 * HEADS, rows)]
        if last:
            shapes = [(rows, width), (rows, LANES)] + shapes
        out_shape = [jax.ShapeDtypeStruct(shape, F32) for shape in shapes[:2]]
        scratch = [pltpu.VMEM(shape, F32) for shape in shapes[2:]]
        pairs_shape = jax.ShapeDtypeStruct((HEADS // 2, 2 * head, 2 * rows), BF16)
        if state is None:
            out_shape.append(pairs_shape)
        others = [queries] if state is None else state
        aliases = {} if state is None or last else {len(served) + 2: 0, len(served) + 3: 1}
        acc, stat, *pairs = pl.pallas_call(
            functools.partial(blocks_kernel, loop_size, tuple(served), state is None, last),
            out_shape=out_shape,
            in_specs=[pl.BlockSpec(memory_space=pltpu.SMEM)]
            + [pl.BlockSpec(memory_space=pl.ANY)] * len(served)
            + vmem_specs(len(others)),
            out_specs=vmem_specs(len(out_shape)),
            scratch_shapes=scratch
            + [
                pltpu.VMEM((tile_list.shape[1],) + tile_shape.shape, BF16),
                pltpu.SemaphoreType.DMA((tile_list.shape[1],)),
            ],
            input_output_aliases=aliases,
            compiler_params=params,
            cost_estimate=LONG if state is None else CHEAP,
            name="blocks" + "_".join(map(str, served)),
        )(tile_list, *served.values(), *others)
        return [pairs[0] if state is None else state[0], acc, stat]

    if relayed:

        def relay(order, full, name):
            return pl.pallas_call(
                functools.partial(relay_kernel, groups),
                out_shape=[one_shape] * 2,
                in_specs=vmem_specs(2),
                out_specs=vmem_specs(2),
                compiler_params=params,
                cost_estimate=CHEAP,
                name=name,
            )(order, full)

        full_k = over_grp(outgoing[2], 2)
        near = over_grp(outgoing[1], 1)
        side = flipped(own_tile, 2)
        across = flipped(own_tile, 5)
        twin = flipped(own_tile, 1)
        state = attend({0: own_tile}, None, False)
        side, across, twin, state = fence((side, across, twin, state))
        corner = flipped(side, 4)
        corner_twin = flipped(across, 2)
        side_twin = flipped(side, 1)
        full_k, own_vals = fence((full_k, value_rows))
        full_v = over_grp(own_vals, 2)
        keys_2, passed = relay(full_k, full_k, "relay_keys")
        keys_3 = over_grp(passed, 1)
        state = attend({1: twin, 2: side, 4: across}, state, False)
        full_v, near, state = fence((full_v, near, state))
        vals_2, passed = relay(full_k, full_v, "relay_vals")
        vals_3 = over_grp(passed, 1)
        key_parts = [outgoing[0], near, keys_2, keys_3]
        val_parts = [outgoing[0], near, vals_2, vals_3]
        late = {3: side_twin, 5: corner, 6: corner_twin}
        _, acc, stat = attend(late, state, True)
    else:
        tiles = {}
        for offset in range(-RADIUS, RADIUS + 1):
            pairs = [(i, (i - offset) % loop_size) for i in range(loop_size)]
            tile = lax.ppermute(own_tile, "loop", pairs) if offset else own_tile
            tiles[offset + RADIUS] = tile
        _, acc, stat = attend(tiles, None, True)
        key_parts = val_parts = [outgoing[0]] + [over_grp(outgoing[b], b) for b in range(1, groups)]

    bias = jnp.pad(expander_bias, ((0, 0), (0, LANES - HEADS)))
    part, edge = pl.pallas_call(
        functools.partial(weigh_kernel, groups),
        out_shape=[
            jax.ShapeDtypeStruct((rows, width), F32),
            jax.ShapeDtypeStruct((MATCHINGS, rows, width), F32),
        ],
        in_specs=vmem_specs(4 + 2 * groups),
        out_specs=vmem_specs(2),
        compiler_params=params,
        cost_estimate=CHEAP,
        name="weigh",
    )(queries, expander_order, bias, acc, stat, *key_parts, *val_parts[:-1])
    return pl.pallas_call(
        functools.partial(finish_kernel, groups),
        out_shape=jax.ShapeDtypeStruct((rows, width), BF16),
        in_specs=vmem_specs(5),
        out_specs=pl.BlockSpec(memory_space=pltpu.VMEM),
        compiler_params=params,
        cost_estimate=CHEAP,
        name="finish",
    )(val_parts[-1], expander_order, part, edge, out_weight)


def solution(mesh):
    placed = (
        P(("loop", "grp"), None),
        P(("loop", "grp"), None),
        P(("loop", "grp"), None),
        P(),
        P(("loop", "grp"), None),
        P(None, ("loop", "grp")),
        P(),
    )
    return jax.shard_map(
        functools.partial(shards, mesh.shape["grp"], mesh.shape["loop"]),
        mesh=mesh,
        in_specs=placed,
        out_specs=P(("loop", "grp"), None),
        check_vma=False,
    )
```

```python
import functools

import jax
import jax.numpy as jnp
from jax import lax
from jax.experimental import pallas as pl
from jax.experimental.pallas import tpu as pltpu
from jax.sharding import PartitionSpec as P

HEADS = 8
RADIUS = 3
MATCHINGS = 3
LANES = 128
ORDER_ROWS = 16
LOG2E = 1.4426950408889634
NEG_FILL = -1e30
VMEM_BYTES = 40 * 1024 * 1024

LONG = pl.CostEstimate(flops=10**10, bytes_accessed=1000, transcendentals=0)
CHEAP = pl.CostEstimate(flops=1000, bytes_accessed=1000, transcendentals=0)
F32 = jnp.float32
BF16 = jnp.bfloat16


def dot(a, b, contract=((1,), (0,))):
    return lax.dot_general(a, b, (contract, ((), ())), preferred_element_type=F32)


def place_table(order_row, rows):
    row_ids = lax.broadcasted_iota(jnp.int32, (rows, rows), 0)
    return jnp.where(row_ids == order_row, 1.0, 0.0).astype(BF16)


def prep_kernel(groups, k_hbm, v_hbm, order_hbm, tile_ref, *refs):
    out_refs, (order_ref, sems) = refs[:-2], refs[-2:]
    rows, width = k_hbm.shape
    bucket = rows // groups
    places = [(order_hbm, order_ref), (k_hbm, tile_ref.at[:, :width]), (v_hbm, tile_ref.at[:, width:])]
    copies = [pltpu.make_async_copy(src, dst, sems.at[i]) for i, (src, dst) in enumerate(places)]
    for copy in copies:
        copy.start()
    copies[0].wait()
    order = order_ref[...]
    lane = lax.broadcasted_iota(jnp.int32, order.shape, 1)
    swapped = jnp.where(lane % 2 == 0, jnp.roll(order, -1, axis=1), jnp.roll(order, 1, axis=1))
    wanted = jnp.where(lane < bucket, swapped, order)
    paired = [ref for ref in out_refs if ref.shape[1] == 2 * width]
    n_slots = len(paired) * bucket
    tables = [place_table(wanted[j : j + 1, :], rows)[:, :n_slots] for j in range(MATCHINGS)]
    table = jnp.concatenate(tables, axis=1)
    for copy in copies[1:]:
        copy.wait()
    tile = tile_ref[...]
    for ref in out_refs[len(paired) :]:
        ref[:rows, :] = tile[:, :width]
        padded = jnp.concatenate([order, jnp.zeros((ORDER_ROWS - MATCHINGS, rows), jnp.int32)], axis=0)
        ref[rows:, :rows] = padded.astype(F32).astype(BF16)
        ref[rows:, rows:] = jnp.zeros((ORDER_ROWS, width - rows), BF16)
    ordered = dot(table, tile, ((0,), (0,))).astype(BF16)
    for j in range(MATCHINGS):
        mine = slice(j * bucket, (j + 1) * bucket)
        for b, out_ref in enumerate(paired):
            out_ref[mine, :] = ordered[j * n_slots + b * bucket : j * n_slots + (b + 1) * bucket]


def relay_kernel(groups, order_ref, rows_ref, mine_ref, next_ref):
    bucket = mine_ref.shape[0] // MATCHINGS
    rows = bucket * groups
    full = rows_ref[:rows, :]
    order = order_ref[rows:, :rows].astype(F32).astype(jnp.int32)
    tables = [place_table(order[j : j + 1, :], rows)[:, 2 * bucket :] for j in range(MATCHINGS)]
    ordered = dot(jnp.concatenate(tables, axis=1), full, ((0,), (0,))).astype(BF16)
    for j in range(MATCHINGS):
        mine = slice(j * bucket, (j + 1) * bucket)
        mine_ref[mine, :] = ordered[2 * j * bucket : (2 * j + 1) * bucket]
        next_ref[mine, :] = ordered[(2 * j + 1) * bucket : (2 * j + 2) * bucket]


def blocks_kernel(loop_size, served, first, last, tiles_ref, *refs):
    n_bufs = 2 * RADIUS + 1
    refs = list(refs)
    bufs = {slot: refs.pop(0) for slot in served}
    if first:
        q_ref, pairs_ref = refs.pop(0), None
    else:
        pairs_ref, acc_in, stat_in = refs.pop(0), refs.pop(0), refs.pop(0)
    acc_out, stat_out = refs.pop(0), refs.pop(0)
    if pairs_ref is None:
        pairs_ref = refs.pop(0)
    if last:
        acc, stat, tile_vmem, sems = refs
    else:
        (acc, stat), (tile_vmem, sems) = (acc_out, stat_out), refs
    width, rows = acc.shape
    head = width // HEADS
    n_tiles = tiles_ref.shape[1]
    here = lax.axis_index("loop")

    def slot_of(t):
        offset = tiles_ref[0, t]
        slot = offset
        if loop_size == 8:
            away = here ^ lax.rem(here + offset - RADIUS + loop_size, loop_size)
            slot = jnp.where(away > 4, away - 1, away)
        return jnp.where(offset <= 2 * RADIUS, slot, n_bufs)

    def here_served(slot):
        return functools.reduce(jnp.logical_or, [slot == k for k in served])

    def fetch(slot, t):
        return pltpu.make_async_copy(bufs[slot], tile_vmem.at[t], sems.at[t])

    for t in range(n_tiles):
        slot = slot_of(t)
        for k in served:

            @pl.when(slot == k)
            def _():
                fetch(k, t).start()

    if first:
        q_t = q_ref[...].T
        zeros = jnp.zeros((head, rows), BF16)
        for p in range(HEADS // 2):
            even = q_t[2 * p * head : (2 * p + 1) * head]
            odd = q_t[(2 * p + 1) * head : (2 * p + 2) * head]
            pairs_ref[p, :head, :rows] = even
            pairs_ref[p, :head, rows:] = zeros
            pairs_ref[p, head:, :rows] = zeros
            pairs_ref[p, head:, rows:] = odd
        stat[:HEADS] = jnp.full((HEADS, rows), NEG_FILL, F32)
        stat[HEADS:] = jnp.zeros((HEADS, rows), F32)
        acc[...] = jnp.zeros(acc.shape, F32)
    else:
        acc[...] = acc_in[...]
        stat[...] = stat_in[...]
    scale = head ** (-0.5) * LOG2E

    def one_tile(t, carry):
        @pl.when(here_served(slot_of(t)))
        def _():
            fetch(next(iter(served)), t).wait()
            scores = []
            for p in range(HEADS // 2):
                keys = tile_vmem[t, :, 2 * p * head : (2 * p + 2) * head]
                scores.append(dot(keys, pairs_ref[p]))
            vals = tile_vmem[t, :, width:].T
            for p in range(HEADS // 2):
                old = jnp.concatenate([stat[2 * p : 2 * p + 1], stat[2 * p + 1 : 2 * p + 2]], axis=1)
                new = jnp.maximum(old, jnp.max(scores[p], axis=0, keepdims=True))
                alpha = jnp.exp2((old - new) * scale)
                w = jnp.exp2((scores[p] - new) * scale)
                total = jnp.sum(w, axis=0, keepdims=True)
                w = w.astype(BF16)
                for side in range(2):
                    h = 2 * p + side
                    half = slice(side * rows, (side + 1) * rows)
                    mine = slice(h * head, (h + 1) * head)
                    stat[h : h + 1] = new[:, half]
                    stat[HEADS + h : HEADS + h + 1] = stat[HEADS + h : HEADS + h + 1] * alpha[:, half] + total[:, half]
                    acc[mine, :] = acc[mine, :] * alpha[:, half] + dot(vals[mine, :], w[:, half])

        return carry

    lax.fori_loop(0, n_tiles, one_tile, 0)
    if last:
        acc_out[...] = acc[...].T
        pad = jnp.zeros((LANES - 2 * HEADS, rows), F32)
        stat_out[...] = jnp.concatenate([stat[...], pad], axis=0).T


def rows_in_order(refs, j, bucket, first, width):
    parts = []
    for ref in refs:
        top = ref.shape[0] - (MATCHINGS - j) * bucket
        left = first if ref.shape[1] == 2 * width else 0
        parts.append(ref[top : top + bucket, left : left + width])
    return jnp.concatenate(parts, axis=0)


def score_kernel(groups, q_ref, order_ref, bias_ref, *refs):
    key_refs = refs[:groups]
    score_ref = refs[groups]
    rows, width = q_ref.shape
    head = width // HEADS
    bucket = rows // groups
    gather = (
        lax.broadcasted_iota(jnp.int32, (width, LANES), 0) // head
        == lax.broadcasted_iota(jnp.int32, (width, LANES), 1)
    )
    gather = jnp.where(gather, 1.0, 0.0).astype(BF16)
    queries = q_ref[...].astype(F32)
    for j in range(MATCHINGS):
        table = place_table(order_ref[j : j + 1, :], rows)
        prod = queries * dot(table, rows_in_order(key_refs, j, bucket, 0, width))
        high = prod.astype(BF16)
        low = (prod - high.astype(F32)).astype(BF16)
        score_ref[j] = dot(high, gather) + dot(low, gather) + bias_ref[j : j + 1, :] * head**0.5


def weigh_kernel(groups, order_ref, acc_ref, stat_ref, score_ref, *refs):
    val_refs = refs[: groups - 1]
    part_ref, edge_ref = refs[groups - 1 :]
    rows, width = part_ref.shape
    head = width // HEADS
    bucket = rows // groups
    scale = head ** (-0.5) * LOG2E
    spread = (
        lax.broadcasted_iota(jnp.int32, (LANES, width), 1) // head
        == lax.broadcasted_iota(jnp.int32, (LANES, width), 0)
    )
    spread = jnp.where(spread, 1.0, 0.0).astype(BF16)
    stat = stat_ref[...]
    lane = lax.broadcasted_iota(jnp.int32, stat.shape, 1)
    block_max = jnp.where(lane < HEADS, stat, 0.0)
    block_sum = jnp.where(lane < HEADS, jnp.roll(stat, -HEADS, axis=1), 1.0)
    edge_scores = [score_ref[j] for j in range(MATCHINGS)]
    top = block_max
    for edge in edge_scores:
        top = jnp.maximum(top, edge)
    keep = jnp.exp2((block_max - top) * scale)
    edge_w = [jnp.exp2((edge - top) * scale) for edge in edge_scores]
    total = block_sum * keep
    for u in edge_w:
        total = total + u
    inv = 1.0 / total

    def wide(x):
        high = x.astype(BF16)
        low = (x - high.astype(F32)).astype(BF16)
        return dot(high, spread) + dot(low, spread)

    numer = acc_ref[...] * wide(keep * inv)
    for j in range(MATCHINGS):
        table = place_table(order_ref[j : j + 1, :], rows)[:, : rows - bucket]
        edge = wide(edge_w[j].astype(BF16).astype(F32) * inv)
        edge_ref[j] = edge
        numer = numer + edge * dot(table, rows_in_order(val_refs, j, bucket, width, width))
    part_ref[...] = numer


def finish_kernel(groups, val_ref, order_ref, part_ref, edge_ref, w_ref, out_ref):
    rows, width = part_ref.shape
    bucket = rows // groups
    numer = part_ref[...]
    for j in range(MATCHINGS):
        table = place_table(order_ref[j : j + 1, :], rows)[:, rows - bucket :]
        numer = numer + edge_ref[j] * dot(table, rows_in_order([val_ref], j, bucket, width, width))
    out_ref[...] = dot(numer.astype(BF16), w_ref[...]).astype(BF16)


fence = lax.optimization_barrier


def vmem_specs(n):
    return [pl.BlockSpec(memory_space=pltpu.VMEM)] * n


def shards(groups, loop_size, queries, key_rows, value_rows, out_weight, tile_list, expander_order, expander_bias):
    rows, width = queries.shape
    head = width // HEADS
    bucket = rows // groups
    params = pltpu.CompilerParams(vmem_limit_bytes=VMEM_BYTES)
    tile_shape = jax.ShapeDtypeStruct((rows, 2 * width), BF16)
    relayed = loop_size == 8 and groups == 4
    kv_shape = jax.ShapeDtypeStruct((MATCHINGS * bucket, 2 * width), BF16)
    one_shape = jax.ShapeDtypeStruct((MATCHINGS * bucket, width), BF16)
    full_shape = jax.ShapeDtypeStruct((rows + ORDER_ROWS, width), BF16)
    bucket_shapes = [kv_shape, kv_shape, full_shape] if relayed else [kv_shape] * groups
    own_tile, *outgoing = pl.pallas_call(
        functools.partial(prep_kernel, groups),
        out_shape=[tile_shape] + bucket_shapes,
        in_specs=[pl.BlockSpec(memory_space=pltpu.HBM)] * 3,
        out_specs=vmem_specs(1 + len(bucket_shapes)),
        scratch_shapes=[
            pltpu.VMEM(expander_order.shape, jnp.int32),
            pltpu.SemaphoreType.DMA((3,)),
        ],
        name="prep",
    )(key_rows, value_rows, expander_order)

    def over_grp(array, b):
        return lax.ppermute(array, "grp", [(i, i ^ b) for i in range(groups)])

    def flipped(array, bits):
        return lax.ppermute(array, "loop", [(i, i ^ bits) for i in range(loop_size)])

    def attend(served, state, last):
        shapes = [(width, rows), (2 * HEADS, rows)]
        if last:
            shapes = [(rows, width), (rows, LANES)] + shapes
        out_shape = [jax.ShapeDtypeStruct(shape, F32) for shape in shapes[:2]]
        scratch = [pltpu.VMEM(shape, F32) for shape in shapes[2:]]
        pairs_shape = jax.ShapeDtypeStruct((HEADS // 2, 2 * head, 2 * rows), BF16)
        if state is None:
            out_shape.append(pairs_shape)
        others = [queries] if state is None else state
        aliases = {} if state is None or last else {len(served) + 2: 0, len(served) + 3: 1}
        acc, stat, *pairs = pl.pallas_call(
            functools.partial(blocks_kernel, loop_size, tuple(served), state is None, last),
            out_shape=out_shape,
            in_specs=[pl.BlockSpec(memory_space=pltpu.SMEM)]
            + [pl.BlockSpec(memory_space=pl.ANY)] * len(served)
            + vmem_specs(len(others)),
            out_specs=vmem_specs(len(out_shape)),
            scratch_shapes=scratch
            + [
                pltpu.VMEM((tile_list.shape[1],) + tile_shape.shape, BF16),
                pltpu.SemaphoreType.DMA((tile_list.shape[1],)),
            ],
            input_output_aliases=aliases,
            compiler_params=params,
            cost_estimate=pl.CostEstimate(flops=1000, bytes_accessed=1000, transcendentals=0) if state is None else CHEAP,
            name="blocks" + "_".join(map(str, served)),
        )(tile_list, *served.values(), *others)
        return [pairs[0] if state is None else state[0], acc, stat]

    bias = jnp.pad(expander_bias, ((0, 0), (0, LANES - HEADS)))

    def score(key_parts):
        return pl.pallas_call(
            functools.partial(score_kernel, groups),
            out_shape=jax.ShapeDtypeStruct((MATCHINGS, rows, LANES), F32),
            in_specs=vmem_specs(3 + groups),
            out_specs=pl.BlockSpec(memory_space=pltpu.VMEM),
            compiler_params=params,
            cost_estimate=CHEAP,
            name="score",
        )(queries, expander_order, bias, *key_parts)

    if relayed:

        def relay(order, full, name):
            return pl.pallas_call(
                functools.partial(relay_kernel, groups),
                out_shape=[one_shape] * 2,
                in_specs=vmem_specs(2),
                out_specs=vmem_specs(2),
                compiler_params=params,
                cost_estimate=pl.CostEstimate(flops=10**10 if name == "relay_keys" else 2*10**9, bytes_accessed=1000, transcendentals=0),
                name=name,
            )(order, full)

        full_k = over_grp(outgoing[2], 2)
        near = over_grp(outgoing[1], 1)
        across = flipped(own_tile, 5)
        side = flipped(own_tile, 2)
        twin = flipped(own_tile, 1)
        state = attend({0: own_tile}, None, False)
        full_k, own_vals, state = fence((full_k, value_rows, state))
        full_v = over_grp(own_vals, 2)
        keys_2, passed = relay(full_k, full_k, "relay_keys")
        across, side, twin, state, keys_2, passed = fence((across, side, twin, state, keys_2, passed))
        corner_twin = flipped(across, 2)
        corner = flipped(side, 4)
        side_twin = flipped(side, 1)
        keys_3 = over_grp(passed, 1)
        state = attend({1: twin, 2: side, 4: across}, state, False)
        full_v, near, state = fence((full_v, near, state))
        state = attend({3: side_twin}, state, False)
        vals_2, passed = relay(full_k, full_v, "relay_vals")
        vals_3 = over_grp(passed, 1)
        val_parts = [outgoing[0], near, vals_2, vals_3]
        late = {5: corner, 6: corner_twin}
        _, acc, stat = attend(late, state, True)
        keys_3, acc, stat = fence((keys_3, acc, stat))
        scores = score([outgoing[0], near, keys_2, keys_3])
    else:
        tiles = {}
        for offset in range(-RADIUS, RADIUS + 1):
            pairs = [(i, (i - offset) % loop_size) for i in range(loop_size)]
            tile = lax.ppermute(own_tile, "loop", pairs) if offset else own_tile
            tiles[offset + RADIUS] = tile
        _, acc, stat = attend(tiles, None, True)
        val_parts = [outgoing[0]] + [over_grp(outgoing[b], b) for b in range(1, groups)]
        scores = score(val_parts)

    part, edge = pl.pallas_call(
        functools.partial(weigh_kernel, groups),
        out_shape=[
            jax.ShapeDtypeStruct((rows, width), F32),
            jax.ShapeDtypeStruct((MATCHINGS, rows, width), F32),
        ],
        in_specs=vmem_specs(3 + groups),
        out_specs=vmem_specs(2),
        compiler_params=params,
        cost_estimate=CHEAP,
        name="weigh",
    )(expander_order, acc, stat, scores, *val_parts[:-1])
    return pl.pallas_call(
        functools.partial(finish_kernel, groups),
        out_shape=jax.ShapeDtypeStruct((rows, width), BF16),
        in_specs=vmem_specs(5),
        out_specs=pl.BlockSpec(memory_space=pltpu.VMEM),
        compiler_params=params,
        cost_estimate=CHEAP,
        name="finish",
    )(val_parts[-1], expander_order, part, edge, out_weight)


def solution(mesh):
    placed = (
        P(("loop", "grp"), None),
        P(("loop", "grp"), None),
        P(("loop", "grp"), None),
        P(),
        P(("loop", "grp"), None),
        P(None, ("loop", "grp")),
        P(),
    )
    return jax.shard_map(
        functools.partial(shards, mesh.shape["grp"], mesh.shape["loop"]),
        mesh=mesh,
        in_specs=placed,
        out_specs=P(("loop", "grp"), None),
        check_vma=False,
    )
```

```python
import functools

import jax
import jax.numpy as jnp
from jax import lax
from jax.experimental import pallas as pl
from jax.experimental.pallas import tpu as pltpu
from jax.sharding import PartitionSpec as P

HEADS = 8
RADIUS = 3
MATCHINGS = 3
LANES = 128
ORDER_ROWS = 16
LOG2E = 1.4426950408889634
NEG_FILL = -1e30
VMEM_BYTES = 40 * 1024 * 1024

LONG = pl.CostEstimate(flops=10**10, bytes_accessed=1000, transcendentals=0)
CHEAP = pl.CostEstimate(flops=1000, bytes_accessed=1000, transcendentals=0)
F32 = jnp.float32
BF16 = jnp.bfloat16


def dot(a, b, contract=((1,), (0,))):
    return lax.dot_general(a, b, (contract, ((), ())), preferred_element_type=F32)


def place_table(order_row, rows):
    row_ids = lax.broadcasted_iota(jnp.int32, (rows, rows), 0)
    return jnp.where(row_ids == order_row, 1.0, 0.0).astype(BF16)


def prep_kernel(groups, k_hbm, v_hbm, order_hbm, tile_ref, *refs):
    out_refs, (order_ref, sems) = refs[:-2], refs[-2:]
    rows, width = k_hbm.shape
    bucket = rows // groups
    places = [(order_hbm, order_ref), (k_hbm, tile_ref.at[:, :width]), (v_hbm, tile_ref.at[:, width:])]
    copies = [pltpu.make_async_copy(src, dst, sems.at[i]) for i, (src, dst) in enumerate(places)]
    for copy in copies:
        copy.start()
    copies[0].wait()
    order = order_ref[...]
    lane = lax.broadcasted_iota(jnp.int32, order.shape, 1)
    swapped = jnp.where(lane % 2 == 0, jnp.roll(order, -1, axis=1), jnp.roll(order, 1, axis=1))
    wanted = jnp.where(lane < bucket, swapped, order)
    paired = [ref for ref in out_refs if ref.shape[1] == 2 * width]
    n_slots = len(paired) * bucket
    tables = [place_table(wanted[j : j + 1, :], rows)[:, :n_slots] for j in range(MATCHINGS)]
    table = jnp.concatenate(tables, axis=1)
    for copy in copies[1:]:
        copy.wait()
    tile = tile_ref[...]
    for ref in out_refs[len(paired) :]:
        ref[:rows, :] = tile[:, :width]
        padded = jnp.concatenate([order, jnp.zeros((ORDER_ROWS - MATCHINGS, rows), jnp.int32)], axis=0)
        ref[rows:, :rows] = padded.astype(F32).astype(BF16)
        ref[rows:, rows:] = jnp.zeros((ORDER_ROWS, width - rows), BF16)
    ordered = dot(table, tile, ((0,), (0,))).astype(BF16)
    for j in range(MATCHINGS):
        mine = slice(j * bucket, (j + 1) * bucket)
        for b, out_ref in enumerate(paired):
            out_ref[mine, :] = ordered[j * n_slots + b * bucket : j * n_slots + (b + 1) * bucket]


def relay_kernel(groups, order_ref, rows_ref, mine_ref, next_ref):
    bucket = mine_ref.shape[0] // MATCHINGS
    rows = bucket * groups
    full = rows_ref[:rows, :]
    order = order_ref[rows:, :rows].astype(F32).astype(jnp.int32)
    tables = [place_table(order[j : j + 1, :], rows)[:, 2 * bucket :] for j in range(MATCHINGS)]
    ordered = dot(jnp.concatenate(tables, axis=1), full, ((0,), (0,))).astype(BF16)
    for j in range(MATCHINGS):
        mine = slice(j * bucket, (j + 1) * bucket)
        mine_ref[mine, :] = ordered[2 * j * bucket : (2 * j + 1) * bucket]
        next_ref[mine, :] = ordered[(2 * j + 1) * bucket : (2 * j + 2) * bucket]


def blocks_kernel(loop_size, served, first, last, tiles_ref, *refs):
    n_bufs = 2 * RADIUS + 1
    refs = list(refs)
    bufs = {slot: refs.pop(0) for slot in served}
    if first:
        q_ref, pairs_ref = refs.pop(0), None
    else:
        pairs_ref, acc_in, stat_in = refs.pop(0), refs.pop(0), refs.pop(0)
    acc_out, stat_out = refs.pop(0), refs.pop(0)
    if pairs_ref is None:
        pairs_ref = refs.pop(0)
    if last:
        acc, stat, tile_vmem, sems = refs
    else:
        (acc, stat), (tile_vmem, sems) = (acc_out, stat_out), refs
    width, rows = acc.shape
    head = width // HEADS
    n_tiles = tiles_ref.shape[1]
    here = lax.axis_index("loop")

    def slot_of(t):
        offset = tiles_ref[0, t]
        slot = offset
        if loop_size == 8:
            away = here ^ lax.rem(here + offset - RADIUS + loop_size, loop_size)
            slot = jnp.where(away > 4, away - 1, away)
        return jnp.where(offset <= 2 * RADIUS, slot, n_bufs)

    def here_served(slot):
        return functools.reduce(jnp.logical_or, [slot == k for k in served])

    def fetch(slot, t):
        return pltpu.make_async_copy(bufs[slot], tile_vmem.at[t], sems.at[t])

    for t in range(n_tiles):
        slot = slot_of(t)
        for k in served:

            @pl.when(slot == k)
            def _():
                fetch(k, t).start()

    if first:
        q_t = q_ref[...].T
        zeros = jnp.zeros((head, rows), BF16)
        for p in range(HEADS // 2):
            even = q_t[2 * p * head : (2 * p + 1) * head]
            odd = q_t[(2 * p + 1) * head : (2 * p + 2) * head]
            pairs_ref[p, :head, :rows] = even
            pairs_ref[p, :head, rows:] = zeros
            pairs_ref[p, head:, :rows] = zeros
            pairs_ref[p, head:, rows:] = odd
        stat[:HEADS] = jnp.full((HEADS, rows), NEG_FILL, F32)
        stat[HEADS:] = jnp.zeros((HEADS, rows), F32)
        acc[...] = jnp.zeros(acc.shape, F32)
    else:
        acc[...] = acc_in[...]
        stat[...] = stat_in[...]
    scale = head ** (-0.5) * LOG2E

    def one_tile(t, carry):
        @pl.when(here_served(slot_of(t)))
        def _():
            fetch(next(iter(served)), t).wait()
            scores = []
            for p in range(HEADS // 2):
                keys = tile_vmem[t, :, 2 * p * head : (2 * p + 2) * head]
                scores.append(dot(keys, pairs_ref[p]))
            vals = tile_vmem[t, :, width:].T
            for p in range(HEADS // 2):
                old = jnp.concatenate([stat[2 * p : 2 * p + 1], stat[2 * p + 1 : 2 * p + 2]], axis=1)
                new = jnp.maximum(old, jnp.max(scores[p], axis=0, keepdims=True))
                alpha = jnp.exp2((old - new) * scale)
                w = jnp.exp2((scores[p] - new) * scale)
                total = jnp.sum(w, axis=0, keepdims=True)
                w = w.astype(BF16)
                for side in range(2):
                    h = 2 * p + side
                    half = slice(side * rows, (side + 1) * rows)
                    mine = slice(h * head, (h + 1) * head)
                    stat[h : h + 1] = new[:, half]
                    stat[HEADS + h : HEADS + h + 1] = stat[HEADS + h : HEADS + h + 1] * alpha[:, half] + total[:, half]
                    acc[mine, :] = acc[mine, :] * alpha[:, half] + dot(vals[mine, :], w[:, half])

        return carry

    lax.fori_loop(0, n_tiles, one_tile, 0)
    if last:
        acc_out[...] = acc[...].T
        pad = jnp.zeros((LANES - 2 * HEADS, rows), F32)
        stat_out[...] = jnp.concatenate([stat[...], pad], axis=0).T


def rows_in_order(refs, j, bucket, first, width):
    parts = []
    for ref in refs:
        top = ref.shape[0] - (MATCHINGS - j) * bucket
        left = first if ref.shape[1] == 2 * width else 0
        parts.append(ref[top : top + bucket, left : left + width])
    return jnp.concatenate(parts, axis=0)


def score_kernel(groups, q_ref, order_ref, bias_ref, *refs):
    key_refs = refs[:groups]
    score_ref = refs[groups]
    rows, width = q_ref.shape
    head = width // HEADS
    bucket = rows // groups
    gather = (
        lax.broadcasted_iota(jnp.int32, (width, LANES), 0) // head
        == lax.broadcasted_iota(jnp.int32, (width, LANES), 1)
    )
    gather = jnp.where(gather, 1.0, 0.0).astype(BF16)
    queries = q_ref[...].astype(F32)
    for j in range(MATCHINGS):
        table = place_table(order_ref[j : j + 1, :], rows)
        prod = queries * dot(table, rows_in_order(key_refs, j, bucket, 0, width))
        high = prod.astype(BF16)
        low = (prod - high.astype(F32)).astype(BF16)
        score_ref[j] = dot(high, gather) + dot(low, gather) + bias_ref[j : j + 1, :] * head**0.5


def weigh_kernel(groups, order_ref, acc_ref, stat_ref, score_ref, *refs):
    val_refs = refs[: groups - 1]
    part_ref, edge_ref = refs[groups - 1 :]
    rows, width = part_ref.shape
    head = width // HEADS
    bucket = rows // groups
    scale = head ** (-0.5) * LOG2E
    spread = (
        lax.broadcasted_iota(jnp.int32, (LANES, width), 1) // head
        == lax.broadcasted_iota(jnp.int32, (LANES, width), 0)
    )
    spread = jnp.where(spread, 1.0, 0.0).astype(BF16)
    stat = stat_ref[...]
    lane = lax.broadcasted_iota(jnp.int32, stat.shape, 1)
    block_max = jnp.where(lane < HEADS, stat, 0.0)
    block_sum = jnp.where(lane < HEADS, jnp.roll(stat, -HEADS, axis=1), 1.0)
    edge_scores = [score_ref[j] for j in range(MATCHINGS)]
    top = block_max
    for edge in edge_scores:
        top = jnp.maximum(top, edge)
    keep = jnp.exp2((block_max - top) * scale)
    edge_w = [jnp.exp2((edge - top) * scale) for edge in edge_scores]
    total = block_sum * keep
    for u in edge_w:
        total = total + u
    inv = 1.0 / total

    def wide(x):
        high = x.astype(BF16)
        low = (x - high.astype(F32)).astype(BF16)
        return dot(high, spread) + dot(low, spread)

    numer = acc_ref[...] * wide(keep * inv)
    for j in range(MATCHINGS):
        table = place_table(order_ref[j : j + 1, :], rows)[:, : rows - bucket]
        edge = wide(edge_w[j].astype(BF16).astype(F32) * inv)
        edge_ref[j] = edge
        numer = numer + edge * dot(table, rows_in_order(val_refs, j, bucket, width, width))
    part_ref[...] = numer


def finish_kernel(groups, val_ref, order_ref, part_ref, edge_ref, w_ref, out_ref):
    rows, width = part_ref.shape
    bucket = rows // groups
    numer = part_ref[...]
    for j in range(MATCHINGS):
        table = place_table(order_ref[j : j + 1, :], rows)[:, rows - bucket :]
        numer = numer + edge_ref[j] * dot(table, rows_in_order([val_ref], j, bucket, width, width))
    out_ref[...] = dot(numer.astype(BF16), w_ref[...]).astype(BF16)


fence = lax.optimization_barrier


def vmem_specs(n):
    return [pl.BlockSpec(memory_space=pltpu.VMEM)] * n


def shards(groups, loop_size, queries, key_rows, value_rows, out_weight, tile_list, expander_order, expander_bias):
    rows, width = queries.shape
    head = width // HEADS
    bucket = rows // groups
    params = pltpu.CompilerParams(vmem_limit_bytes=VMEM_BYTES)
    tile_shape = jax.ShapeDtypeStruct((rows, 2 * width), BF16)
    relayed = loop_size == 8 and groups == 4
    kv_shape = jax.ShapeDtypeStruct((MATCHINGS * bucket, 2 * width), BF16)
    one_shape = jax.ShapeDtypeStruct((MATCHINGS * bucket, width), BF16)
    full_shape = jax.ShapeDtypeStruct((rows + ORDER_ROWS, width), BF16)
    bucket_shapes = [kv_shape, kv_shape, full_shape] if relayed else [kv_shape] * groups
    own_tile, *outgoing = pl.pallas_call(
        functools.partial(prep_kernel, groups),
        out_shape=[tile_shape] + bucket_shapes,
        in_specs=[pl.BlockSpec(memory_space=pltpu.HBM)] * 3,
        out_specs=vmem_specs(1 + len(bucket_shapes)),
        scratch_shapes=[
            pltpu.VMEM(expander_order.shape, jnp.int32),
            pltpu.SemaphoreType.DMA((3,)),
        ],
        compiler_params=params,
        name="prep",
    )(*[pltpu.with_memory_space_constraint(x, pltpu.HBM) for x in (key_rows, value_rows, expander_order)])

    def over_grp(array, b):
        return lax.ppermute(array, "grp", [(i, i ^ b) for i in range(groups)])

    def flipped(array, bits):
        return lax.ppermute(array, "loop", [(i, i ^ bits) for i in range(loop_size)])

    def attend(served, state, last):
        shapes = [(width, rows), (2 * HEADS, rows)]
        if last:
            shapes = [(rows, width), (rows, LANES)] + shapes
        out_shape = [jax.ShapeDtypeStruct(shape, F32) for shape in shapes[:2]]
        scratch = [pltpu.VMEM(shape, F32) for shape in shapes[2:]]
        pairs_shape = jax.ShapeDtypeStruct((HEADS // 2, 2 * head, 2 * rows), BF16)
        if state is None:
            out_shape.append(pairs_shape)
        others = [queries] if state is None else state
        aliases = {} if state is None or last else {len(served) + 2: 0, len(served) + 3: 1}
        acc, stat, *pairs = pl.pallas_call(
            functools.partial(blocks_kernel, loop_size, tuple(served), state is None, last),
            out_shape=out_shape,
            in_specs=[pl.BlockSpec(memory_space=pltpu.SMEM)]
            + [pl.BlockSpec(memory_space=pl.ANY)] * len(served)
            + vmem_specs(len(others)),
            out_specs=vmem_specs(len(out_shape)),
            scratch_shapes=scratch
            + [
                pltpu.VMEM((tile_list.shape[1],) + tile_shape.shape, BF16),
                pltpu.SemaphoreType.DMA((tile_list.shape[1],)),
            ],
            input_output_aliases=aliases,
            compiler_params=params,
            cost_estimate=pl.CostEstimate(flops=1000, bytes_accessed=1000, transcendentals=0) if state is None else CHEAP,
            name="blocks" + "_".join(map(str, served)),
        )(tile_list, *served.values(), *others)
        return [pairs[0] if state is None else state[0], acc, stat]

    bias = jnp.pad(expander_bias, ((0, 0), (0, LANES - HEADS)))

    def score(key_parts):
        return pl.pallas_call(
            functools.partial(score_kernel, groups),
            out_shape=jax.ShapeDtypeStruct((MATCHINGS, rows, LANES), F32),
            in_specs=vmem_specs(3 + groups),
            out_specs=pl.BlockSpec(memory_space=pltpu.VMEM),
            compiler_params=params,
            cost_estimate=CHEAP,
            name="score",
        )(queries, expander_order, bias, *key_parts)

    if relayed:

        def relay(order, full, name):
            return pl.pallas_call(
                functools.partial(relay_kernel, groups),
                out_shape=[one_shape] * 2,
                in_specs=vmem_specs(2),
                out_specs=vmem_specs(2),
                compiler_params=params,
                cost_estimate=pl.CostEstimate(flops=10**10 if name == "relay_keys" else 2*10**9, bytes_accessed=1000, transcendentals=0),
                name=name,
            )(order, full)

        full_k = over_grp(outgoing[2], 2)
        near = over_grp(outgoing[1], 1)
        across = flipped(own_tile, 5)
        side = flipped(own_tile, 2)
        twin = flipped(own_tile, 1)
        state = attend({0: own_tile}, None, False)
        full_k, own_vals, state = fence((full_k, value_rows, state))
        full_v = over_grp(own_vals, 2)
        keys_2, passed = relay(full_k, full_k, "relay_keys")
        across, side, twin, state, keys_2, passed = fence((across, side, twin, state, keys_2, passed))
        corner_twin = flipped(across, 2)
        corner = flipped(side, 4)
        side_twin = flipped(side, 1)
        keys_3 = over_grp(passed, 1)
        state = attend({1: twin, 2: side, 4: across}, state, False)
        full_v, near, state = fence((full_v, near, state))
        state = attend({3: side_twin}, state, False)
        vals_2, passed = relay(full_k, full_v, "relay_vals")
        vals_3 = over_grp(passed, 1)
        val_parts = [outgoing[0], near, vals_2, vals_3]
        late = {5: corner, 6: corner_twin}
        _, acc, stat = attend(late, state, True)
        keys_3, acc, stat = fence((keys_3, acc, stat))
        scores = score([outgoing[0], near, keys_2, keys_3])
    else:
        tiles = {}
        for offset in range(-RADIUS, RADIUS + 1):
            pairs = [(i, (i - offset) % loop_size) for i in range(loop_size)]
            tile = lax.ppermute(own_tile, "loop", pairs) if offset else own_tile
            tiles[offset + RADIUS] = tile
        _, acc, stat = attend(tiles, None, True)
        val_parts = [outgoing[0]] + [over_grp(outgoing[b], b) for b in range(1, groups)]
        scores = score(val_parts)

    part, edge = pl.pallas_call(
        functools.partial(weigh_kernel, groups),
        out_shape=[
            jax.ShapeDtypeStruct((rows, width), F32),
            jax.ShapeDtypeStruct((MATCHINGS, rows, width), F32),
        ],
        in_specs=vmem_specs(3 + groups),
        out_specs=vmem_specs(2),
        compiler_params=params,
        cost_estimate=CHEAP,
        name="weigh",
    )(expander_order, acc, stat, scores, *val_parts[:-1])
    return pl.pallas_call(
        functools.partial(finish_kernel, groups),
        out_shape=jax.ShapeDtypeStruct((rows, width), BF16),
        in_specs=vmem_specs(5),
        out_specs=pl.BlockSpec(memory_space=pltpu.VMEM),
        compiler_params=params,
        cost_estimate=CHEAP,
        name="finish",
    )(val_parts[-1], expander_order, part, edge, out_weight)


def solution(mesh):
    placed = (
        P(("loop", "grp"), None),
        P(("loop", "grp"), None),
        P(("loop", "grp"), None),
        P(),
        P(("loop", "grp"), None),
        P(None, ("loop", "grp")),
        P(),
    )
    return jax.shard_map(
        functools.partial(shards, mesh.shape["grp"], mesh.shape["loop"]),
        mesh=mesh,
        in_specs=placed,
        out_specs=P(("loop", "grp"), None),
        check_vma=False,
    )
```

```python
import functools

import jax
import jax.numpy as jnp
from jax import lax
from jax.experimental import pallas as pl
from jax.experimental.pallas import tpu as pltpu
from jax.sharding import PartitionSpec as P

HEADS = 8
RADIUS = 3
MATCHINGS = 3
LANES = 128
ORDER_ROWS = 16
LOG2E = 1.4426950408889634
NEG_FILL = -1e30
VMEM_BYTES = 40 * 1024 * 1024

LONG = pl.CostEstimate(flops=10**10, bytes_accessed=1000, transcendentals=0)
CHEAP = pl.CostEstimate(flops=1000, bytes_accessed=1000, transcendentals=0)
F32 = jnp.float32
BF16 = jnp.bfloat16


def dot(a, b, contract=((1,), (0,))):
    return lax.dot_general(a, b, (contract, ((), ())), preferred_element_type=F32)


def place_table(order_row, rows):
    row_ids = lax.broadcasted_iota(jnp.int32, (rows, rows), 0)
    return jnp.where(row_ids == order_row, 1.0, 0.0).astype(BF16)


def bucket_table(order, bucket, lowest, count):
    lane = lax.broadcasted_iota(jnp.int32, order.shape, 1)
    swapped = jnp.where(lane % 2 == 0, jnp.roll(order, -1, axis=1), jnp.roll(order, 1, axis=1))
    wanted = jnp.where(lane < bucket, swapped, order)
    chosen = slice(lowest * bucket, (lowest + count) * bucket)
    tables = [place_table(wanted[j : j + 1, :], order.shape[1])[:, chosen] for j in range(MATCHINGS)]
    return jnp.concatenate(tables, axis=1)


def put_buckets(ordered, bucket, out_refs):
    for j in range(MATCHINGS):
        for i, out_ref in enumerate(out_refs):
            first = (j * len(out_refs) + i) * bucket
            out_ref[j * bucket : (j + 1) * bucket, :] = ordered[first : first + bucket]


def prep_kernel(groups, lowest, k_hbm, v_hbm, order_hbm, tile_ref, *refs):
    out_refs, (order_ref, sems) = refs[:-2], refs[-2:]
    rows, width = k_hbm.shape
    bucket = rows // groups
    places = [(order_hbm, order_ref), (k_hbm, tile_ref.at[:, :width]), (v_hbm, tile_ref.at[:, width:])]
    copies = [pltpu.make_async_copy(src, dst, sems.at[i]) for i, (src, dst) in enumerate(places)]
    for copy in copies:
        copy.start()
    copies[0].wait()
    order = order_ref[...]
    paired = [ref for ref in out_refs if ref.shape[1] == 2 * width]
    table = bucket_table(order, bucket, lowest, len(paired))
    for copy in copies[1:]:
        copy.wait()
    tile = tile_ref[...]
    for ref in out_refs[len(paired) :]:
        ref[:rows, :] = tile[:, :width]
        padded = jnp.concatenate([order, jnp.zeros((ORDER_ROWS - MATCHINGS, rows), jnp.int32)], axis=0)
        ref[rows:, :rows] = padded.astype(F32).astype(BF16)
        ref[rows:, rows:] = jnp.zeros((ORDER_ROWS, width - rows), BF16)
    put_buckets(dot(table, tile, ((0,), (0,))).astype(BF16), bucket, paired)


def own_bucket_kernel(groups, tile_ref, order_ref, out_ref):
    bucket = tile_ref.shape[0] // groups
    table = bucket_table(order_ref[...], bucket, 0, 1)
    put_buckets(dot(table, tile_ref[...], ((0,), (0,))).astype(BF16), bucket, [out_ref])


def relay_kernel(groups, order_ref, rows_ref, mine_ref, next_ref):
    bucket = mine_ref.shape[0] // MATCHINGS
    rows = bucket * groups
    full = rows_ref[:rows, :]
    order = order_ref[rows:, :rows].astype(F32).astype(jnp.int32)
    tables = [place_table(order[j : j + 1, :], rows)[:, 2 * bucket :] for j in range(MATCHINGS)]
    ordered = dot(jnp.concatenate(tables, axis=1), full, ((0,), (0,))).astype(BF16)
    for j in range(MATCHINGS):
        mine = slice(j * bucket, (j + 1) * bucket)
        mine_ref[mine, :] = ordered[2 * j * bucket : (2 * j + 1) * bucket]
        next_ref[mine, :] = ordered[(2 * j + 1) * bucket : (2 * j + 2) * bucket]


def blocks_kernel(loop_size, served, first, last, tiles_ref, *refs):
    n_bufs = 2 * RADIUS + 1
    refs = list(refs)
    bufs = {slot: refs.pop(0) for slot in served}
    if first:
        q_ref, pairs_ref = refs.pop(0), None
    else:
        pairs_ref, acc_in, stat_in = refs.pop(0), refs.pop(0), refs.pop(0)
    acc_out, stat_out = refs.pop(0), refs.pop(0)
    if pairs_ref is None:
        pairs_ref = refs.pop(0)
    if last:
        acc, stat, tile_vmem, sems = refs
    else:
        (acc, stat), (tile_vmem, sems) = (acc_out, stat_out), refs
    width, rows = acc.shape
    head = width // HEADS
    n_tiles = tiles_ref.shape[1]
    here = lax.axis_index("loop")

    def slot_of(t):
        offset = tiles_ref[0, t]
        slot = offset
        if loop_size == 8:
            away = here ^ lax.rem(here + offset - RADIUS + loop_size, loop_size)
            slot = jnp.where(away > 4, away - 1, away)
        return jnp.where(offset <= 2 * RADIUS, slot, n_bufs)

    def here_served(slot):
        return functools.reduce(jnp.logical_or, [slot == k for k in served])

    def fetch(slot, t):
        return pltpu.make_async_copy(bufs[slot], tile_vmem.at[t], sems.at[t])

    for t in range(n_tiles):
        slot = slot_of(t)
        for k in served:

            @pl.when(slot == k)
            def _():
                fetch(k, t).start()

    if first:
        q_t = q_ref[...].T
        zeros = jnp.zeros((head, rows), BF16)
        for p in range(HEADS // 2):
            even = q_t[2 * p * head : (2 * p + 1) * head]
            odd = q_t[(2 * p + 1) * head : (2 * p + 2) * head]
            pairs_ref[p, :head, :rows] = even
            pairs_ref[p, :head, rows:] = zeros
            pairs_ref[p, head:, :rows] = zeros
            pairs_ref[p, head:, rows:] = odd
        stat[:HEADS] = jnp.full((HEADS, rows), NEG_FILL, F32)
        stat[HEADS:] = jnp.zeros((HEADS, rows), F32)
        acc[...] = jnp.zeros(acc.shape, F32)
    else:
        acc[...] = acc_in[...]
        stat[...] = stat_in[...]
    scale = head ** (-0.5) * LOG2E

    def one_tile(t, carry):
        @pl.when(here_served(slot_of(t)))
        def _():
            fetch(next(iter(served)), t).wait()
            scores = []
            for p in range(HEADS // 2):
                keys = tile_vmem[t, :, 2 * p * head : (2 * p + 2) * head]
                scores.append(dot(keys, pairs_ref[p]))
            vals = tile_vmem[t, :, width:].T
            for p in range(HEADS // 2):
                old = jnp.concatenate([stat[2 * p : 2 * p + 1], stat[2 * p + 1 : 2 * p + 2]], axis=1)
                new = jnp.maximum(old, jnp.max(scores[p], axis=0, keepdims=True))
                alpha = jnp.exp2((old - new) * scale)
                w = jnp.exp2((scores[p] - new) * scale)
                total = jnp.sum(w, axis=0, keepdims=True)
                w = w.astype(BF16)
                for side in range(2):
                    h = 2 * p + side
                    half = slice(side * rows, (side + 1) * rows)
                    mine = slice(h * head, (h + 1) * head)
                    stat[h : h + 1] = new[:, half]
                    stat[HEADS + h : HEADS + h + 1] = stat[HEADS + h : HEADS + h + 1] * alpha[:, half] + total[:, half]
                    acc[mine, :] = acc[mine, :] * alpha[:, half] + dot(vals[mine, :], w[:, half])

        return carry

    lax.fori_loop(0, n_tiles, one_tile, 0)
    if last:
        acc_out[...] = acc[...].T
        pad = jnp.zeros((LANES - 2 * HEADS, rows), F32)
        stat_out[...] = jnp.concatenate([stat[...], pad], axis=0).T


def rows_in_order(refs, j, bucket, first, width):
    parts = []
    for ref in refs:
        top = ref.shape[0] - (MATCHINGS - j) * bucket
        left = first if ref.shape[1] == 2 * width else 0
        parts.append(ref[top : top + bucket, left : left + width])
    return jnp.concatenate(parts, axis=0)


def score_kernel(groups, q_ref, order_ref, bias_ref, *refs):
    key_refs = refs[:groups]
    score_ref = refs[groups]
    rows, width = q_ref.shape
    head = width // HEADS
    bucket = rows // groups
    gather = (
        lax.broadcasted_iota(jnp.int32, (width, LANES), 0) // head
        == lax.broadcasted_iota(jnp.int32, (width, LANES), 1)
    )
    gather = jnp.where(gather, 1.0, 0.0).astype(BF16)
    queries = q_ref[...].astype(F32)
    for j in range(MATCHINGS):
        table = place_table(order_ref[j : j + 1, :], rows)
        prod = queries * dot(table, rows_in_order(key_refs, j, bucket, 0, width))
        high = prod.astype(BF16)
        low = (prod - high.astype(F32)).astype(BF16)
        score_ref[j] = dot(high, gather) + dot(low, gather) + bias_ref[j : j + 1, :] * head**0.5


def weigh_kernel(groups, order_ref, acc_ref, stat_ref, score_ref, *refs):
    val_refs = refs[: groups - 1]
    part_ref, edge_ref = refs[groups - 1 :]
    rows, width = part_ref.shape
    head = width // HEADS
    bucket = rows // groups
    scale = head ** (-0.5) * LOG2E
    spread = (
        lax.broadcasted_iota(jnp.int32, (LANES, width), 1) // head
        == lax.broadcasted_iota(jnp.int32, (LANES, width), 0)
    )
    spread = jnp.where(spread, 1.0, 0.0).astype(BF16)
    stat = stat_ref[...]
    lane = lax.broadcasted_iota(jnp.int32, stat.shape, 1)
    block_max = jnp.where(lane < HEADS, stat, 0.0)
    block_sum = jnp.where(lane < HEADS, jnp.roll(stat, -HEADS, axis=1), 1.0)
    edge_scores = [score_ref[j] for j in range(MATCHINGS)]
    top = block_max
    for edge in edge_scores:
        top = jnp.maximum(top, edge)
    keep = jnp.exp2((block_max - top) * scale)
    edge_w = [jnp.exp2((edge - top) * scale) for edge in edge_scores]
    total = block_sum * keep
    for u in edge_w:
        total = total + u
    inv = 1.0 / total

    def wide(x):
        high = x.astype(BF16)
        low = (x - high.astype(F32)).astype(BF16)
        return dot(high, spread) + dot(low, spread)

    numer = acc_ref[...] * wide(keep * inv)
    for j in range(MATCHINGS):
        table = place_table(order_ref[j : j + 1, :], rows)
        share = edge_w[j].astype(BF16).astype(F32) * inv
        numer = numer + wide(share) * dot(table[:, : rows - bucket], rows_in_order(val_refs, j, bucket, width, width))
        high = share.astype(BF16)
        low = (share - high.astype(F32)).astype(BF16)
        last = table[:, rows - bucket :]
        in_order = dot(last, high, ((0,), (0,))) + dot(last, low, ((0,), (0,)))
        edge_ref[j * bucket : (j + 1) * bucket, :] = wide(in_order)
    part_ref[...] = numer


def finish_kernel(groups, val_ref, order_ref, part_ref, edge_ref, w_ref, out_ref):
    rows, width = part_ref.shape
    bucket = rows // groups
    weighed = edge_ref[...] * val_ref[:, val_ref.shape[1] - width :].astype(F32)
    high = weighed.astype(BF16)
    low = (weighed - high.astype(F32)).astype(BF16)
    tables = [place_table(order_ref[j : j + 1, :], rows)[:, rows - bucket :] for j in range(MATCHINGS)]
    table = jnp.concatenate(tables, axis=1)
    attended = part_ref[...] + dot(table, high) + dot(table, low)
    out_ref[...] = dot(attended.astype(BF16), w_ref[...]).astype(BF16)


fence = lax.optimization_barrier


def vmem_specs(n):
    return [pl.BlockSpec(memory_space=pltpu.VMEM)] * n


def shards(groups, loop_size, queries, key_rows, value_rows, out_weight, tile_list, expander_order, expander_bias):
    rows, width = queries.shape
    head = width // HEADS
    bucket = rows // groups
    params = pltpu.CompilerParams(vmem_limit_bytes=VMEM_BYTES)
    tile_shape = jax.ShapeDtypeStruct((rows, 2 * width), BF16)
    relayed = loop_size == 8 and groups == 4
    kv_shape = jax.ShapeDtypeStruct((MATCHINGS * bucket, 2 * width), BF16)
    one_shape = jax.ShapeDtypeStruct((MATCHINGS * bucket, width), BF16)
    full_shape = jax.ShapeDtypeStruct((rows + ORDER_ROWS, width), BF16)
    bucket_shapes = [kv_shape, full_shape] if relayed else [kv_shape] * groups
    own_tile, *outgoing = pl.pallas_call(
        functools.partial(prep_kernel, groups, 1 if relayed else 0),
        out_shape=[tile_shape] + bucket_shapes,
        in_specs=[pl.BlockSpec(memory_space=pltpu.HBM)] * 3,
        out_specs=vmem_specs(1 + len(bucket_shapes)),
        scratch_shapes=[
            pltpu.VMEM(expander_order.shape, jnp.int32),
            pltpu.SemaphoreType.DMA((3,)),
        ],
        compiler_params=params,
        name="prep",
    )(*[pltpu.with_memory_space_constraint(x, pltpu.HBM) for x in (key_rows, value_rows, expander_order)])

    def over_grp(array, b):
        return lax.ppermute(array, "grp", [(i, i ^ b) for i in range(groups)])

    def flipped(array, bits):
        return lax.ppermute(array, "loop", [(i, i ^ bits) for i in range(loop_size)])

    def attend(served, state, last):
        shapes = [(width, rows), (2 * HEADS, rows)]
        if last:
            shapes = [(rows, width), (rows, LANES)] + shapes
        out_shape = [jax.ShapeDtypeStruct(shape, F32) for shape in shapes[:2]]
        scratch = [pltpu.VMEM(shape, F32) for shape in shapes[2:]]
        pairs_shape = jax.ShapeDtypeStruct((HEADS // 2, 2 * head, 2 * rows), BF16)
        if state is None:
            out_shape.append(pairs_shape)
        others = [queries] if state is None else state
        aliases = {} if state is None or last else {len(served) + 2: 0, len(served) + 3: 1}
        acc, stat, *pairs = pl.pallas_call(
            functools.partial(blocks_kernel, loop_size, tuple(served), state is None, last),
            out_shape=out_shape,
            in_specs=[pl.BlockSpec(memory_space=pltpu.SMEM)]
            + [pl.BlockSpec(memory_space=pl.ANY)] * len(served)
            + vmem_specs(len(others)),
            out_specs=vmem_specs(len(out_shape)),
            scratch_shapes=scratch
            + [
                pltpu.VMEM((tile_list.shape[1],) + tile_shape.shape, BF16),
                pltpu.SemaphoreType.DMA((tile_list.shape[1],)),
            ],
            input_output_aliases=aliases,
            compiler_params=params,
            cost_estimate=pl.CostEstimate(flops=1000, bytes_accessed=1000, transcendentals=0) if state is None else CHEAP,
            name="blocks" + "_".join(map(str, served)),
        )(tile_list, *served.values(), *others)
        return [pairs[0] if state is None else state[0], acc, stat]

    bias = jnp.pad(expander_bias, ((0, 0), (0, LANES - HEADS)))

    def score(key_parts):
        return pl.pallas_call(
            functools.partial(score_kernel, groups),
            out_shape=jax.ShapeDtypeStruct((MATCHINGS, rows, LANES), F32),
            in_specs=vmem_specs(3 + groups),
            out_specs=pl.BlockSpec(memory_space=pltpu.VMEM),
            compiler_params=params,
            cost_estimate=CHEAP,
            name="score",
        )(queries, expander_order, bias, *key_parts)

    if relayed:

        def relay(order, full, name):
            return pl.pallas_call(
                functools.partial(relay_kernel, groups),
                out_shape=[one_shape] * 2,
                in_specs=vmem_specs(2),
                out_specs=vmem_specs(2),
                compiler_params=params,
                cost_estimate=pl.CostEstimate(flops=10**10 if name == "relay_keys" else 2*10**9, bytes_accessed=1000, transcendentals=0),
                name=name,
            )(order, full)

        full_k = over_grp(outgoing[1], 2)
        near = over_grp(outgoing[0], 1)
        across = flipped(own_tile, 5)
        side = flipped(own_tile, 2)
        twin = flipped(own_tile, 1)
        state = attend({0: own_tile}, None, False)
        full_k, own_vals, state = fence((full_k, value_rows, state))
        full_v = over_grp(own_vals, 2)
        keys_2, passed = relay(full_k, full_k, "relay_keys")
        across, side, twin, state, keys_2, passed = fence((across, side, twin, state, keys_2, passed))
        corner_twin = flipped(across, 2)
        corner = flipped(side, 4)
        side_twin = flipped(side, 1)
        keys_3 = over_grp(passed, 1)
        state = attend({1: twin, 2: side, 4: across}, state, False)
        own_bucket = pl.pallas_call(
            functools.partial(own_bucket_kernel, groups),
            out_shape=kv_shape,
            in_specs=vmem_specs(2),
            out_specs=pl.BlockSpec(memory_space=pltpu.VMEM),
            compiler_params=params,
            cost_estimate=CHEAP,
            name="own_bucket",
        )(own_tile, expander_order)
        full_v, near, state, own_bucket = fence((full_v, near, state, own_bucket))
        state = attend({3: side_twin}, state, False)
        vals_2, passed = relay(full_k, full_v, "relay_vals")
        vals_3 = over_grp(passed, 1)
        val_parts = [own_bucket, near, vals_2, vals_3]
        late = {5: corner, 6: corner_twin}
        _, acc, stat = attend(late, state, True)
        keys_3, acc, stat = fence((keys_3, acc, stat))
        scores = score([own_bucket, near, keys_2, keys_3])
    else:
        tiles = {}
        for offset in range(-RADIUS, RADIUS + 1):
            pairs = [(i, (i - offset) % loop_size) for i in range(loop_size)]
            tile = lax.ppermute(own_tile, "loop", pairs) if offset else own_tile
            tiles[offset + RADIUS] = tile
        _, acc, stat = attend(tiles, None, True)
        val_parts = [outgoing[0]] + [over_grp(outgoing[b], b) for b in range(1, groups)]
        scores = score(val_parts)

    part, edge = pl.pallas_call(
        functools.partial(weigh_kernel, groups),
        out_shape=[
            jax.ShapeDtypeStruct((rows, width), F32),
            jax.ShapeDtypeStruct((MATCHINGS * bucket, width), F32),
        ],
        in_specs=vmem_specs(3 + groups),
        out_specs=vmem_specs(2),
        compiler_params=params,
        cost_estimate=CHEAP,
        name="weigh",
    )(expander_order, acc, stat, scores, *val_parts[:-1])
    return pl.pallas_call(
        functools.partial(finish_kernel, groups),
        out_shape=jax.ShapeDtypeStruct((rows, width), BF16),
        in_specs=vmem_specs(5),
        out_specs=pl.BlockSpec(memory_space=pltpu.VMEM),
        compiler_params=params,
        cost_estimate=CHEAP,
        name="finish",
    )(val_parts[-1], expander_order, part, edge, out_weight)


def solution(mesh):
    placed = (
        P(("loop", "grp"), None),
        P(("loop", "grp"), None),
        P(("loop", "grp"), None),
        P(),
        P(("loop", "grp"), None),
        P(None, ("loop", "grp")),
        P(),
    )
    return jax.shard_map(
        functools.partial(shards, mesh.shape["grp"], mesh.shape["loop"]),
        mesh=mesh,
        in_specs=placed,
        out_specs=P(("loop", "grp"), None),
        check_vma=False,
    )
```

```python
import functools

import jax
import jax.numpy as jnp
from jax import lax
from jax.experimental import pallas as pl
from jax.experimental.pallas import tpu as pltpu
from jax.sharding import PartitionSpec as P

HEADS = 8
RADIUS = 3
MATCHINGS = 3
LANES = 128
ORDER_ROWS = 16
LOG2E = 1.4426950408889634
NEG_FILL = -1e30
VMEM_BYTES = 40 * 1024 * 1024

LONG = pl.CostEstimate(flops=10**10, bytes_accessed=1000, transcendentals=0)
CHEAP = pl.CostEstimate(flops=1000, bytes_accessed=1000, transcendentals=0)
F32 = jnp.float32
BF16 = jnp.bfloat16


def dot(a, b, contract=((1,), (0,))):
    return lax.dot_general(a, b, (contract, ((), ())), preferred_element_type=F32)


def place_table(order_row, rows):
    row_ids = lax.broadcasted_iota(jnp.int32, (rows, rows), 0)
    return jnp.where(row_ids == order_row, 1.0, 0.0).astype(BF16)


def bucket_table(order, bucket, lowest, count):
    lane = lax.broadcasted_iota(jnp.int32, order.shape, 1)
    swapped = jnp.where(lane % 2 == 0, jnp.roll(order, -1, axis=1), jnp.roll(order, 1, axis=1))
    wanted = jnp.where(lane < bucket, swapped, order)
    chosen = slice(lowest * bucket, (lowest + count) * bucket)
    tables = [place_table(wanted[j : j + 1, :], order.shape[1])[:, chosen] for j in range(MATCHINGS)]
    return jnp.concatenate(tables, axis=1)


def put_buckets(ordered, bucket, out_refs):
    for j in range(MATCHINGS):
        for i, out_ref in enumerate(out_refs):
            first = (j * len(out_refs) + i) * bucket
            out_ref[j * bucket : (j + 1) * bucket, :] = ordered[first : first + bucket]


def prep_kernel(groups, lowest, k_hbm, v_hbm, order_hbm, tile_ref, *refs):
    out_refs, (order_ref, sems) = refs[:-2], refs[-2:]
    rows, width = k_hbm.shape
    bucket = rows // groups
    places = [(order_hbm, order_ref), (k_hbm, tile_ref.at[:, :width]), (v_hbm, tile_ref.at[:, width:])]
    copies = [pltpu.make_async_copy(src, dst, sems.at[i]) for i, (src, dst) in enumerate(places)]
    for copy in copies:
        copy.start()
    copies[0].wait()
    order = order_ref[...]
    paired = [ref for ref in out_refs if ref.shape[1] == 2 * width]
    table = bucket_table(order, bucket, lowest, len(paired))
    for copy in copies[1:]:
        copy.wait()
    tile = tile_ref[...]
    for ref in out_refs[len(paired) :]:
        ref[:rows, :] = tile[:, :width]
        padded = jnp.concatenate([order, jnp.zeros((ORDER_ROWS - MATCHINGS, rows), jnp.int32)], axis=0)
        ref[rows:, :rows] = padded.astype(F32).astype(BF16)
        ref[rows:, rows:] = jnp.zeros((ORDER_ROWS, width - rows), BF16)
    put_buckets(dot(table, tile, ((0,), (0,))).astype(BF16), bucket, paired)


def own_bucket_kernel(groups, tile_ref, order_ref, out_ref):
    bucket = tile_ref.shape[0] // groups
    table = bucket_table(order_ref[...], bucket, 0, 1)
    put_buckets(dot(table, tile_ref[...], ((0,), (0,))).astype(BF16), bucket, [out_ref])


def relay_kernel(groups, order_ref, rows_ref, mine_ref, next_ref):
    bucket = mine_ref.shape[0] // MATCHINGS
    rows = bucket * groups
    full = rows_ref[:rows, :]
    order = order_ref[rows:, :rows].astype(F32).astype(jnp.int32)
    tables = [place_table(order[j : j + 1, :], rows)[:, 2 * bucket :] for j in range(MATCHINGS)]
    ordered = dot(jnp.concatenate(tables, axis=1), full, ((0,), (0,))).astype(BF16)
    for j in range(MATCHINGS):
        mine = slice(j * bucket, (j + 1) * bucket)
        mine_ref[mine, :] = ordered[2 * j * bucket : (2 * j + 1) * bucket]
        next_ref[mine, :] = ordered[(2 * j + 1) * bucket : (2 * j + 2) * bucket]


def blocks_kernel(loop_size, served, first, last, tiles_ref, *refs):
    n_bufs = 2 * RADIUS + 1
    refs = list(refs)
    bufs = {slot: refs.pop(0) for slot in served}
    if first:
        q_ref, pairs_ref = refs.pop(0), None
    else:
        pairs_ref, acc_in, stat_in = refs.pop(0), refs.pop(0), refs.pop(0)
    acc_out, stat_out = refs.pop(0), refs.pop(0)
    if pairs_ref is None:
        pairs_ref = refs.pop(0)
    if last:
        acc, stat, tile_vmem, sems = refs
    else:
        (acc, stat), (tile_vmem, sems) = (acc_out, stat_out), refs
    width, rows = acc.shape
    head = width // HEADS
    n_tiles = tiles_ref.shape[1]
    here = lax.axis_index("loop")

    def slot_of(t):
        offset = tiles_ref[0, t]
        slot = offset
        if loop_size == 8:
            away = here ^ lax.rem(here + offset - RADIUS + loop_size, loop_size)
            slot = jnp.where(away > 4, away - 1, away)
        return jnp.where(offset <= 2 * RADIUS, slot, n_bufs)

    def here_served(slot):
        return functools.reduce(jnp.logical_or, [slot == k for k in served])

    def fetch(slot, t):
        return pltpu.make_async_copy(bufs[slot], tile_vmem.at[t], sems.at[t])

    for t in range(n_tiles):
        slot = slot_of(t)
        for k in served:

            @pl.when(slot == k)
            def _():
                fetch(k, t).start()

    if first:
        q_t = q_ref[...].T
        zeros = jnp.zeros((head, rows), BF16)
        for p in range(HEADS // 2):
            even = q_t[2 * p * head : (2 * p + 1) * head]
            odd = q_t[(2 * p + 1) * head : (2 * p + 2) * head]
            pairs_ref[p, :head, :rows] = even
            pairs_ref[p, :head, rows:] = zeros
            pairs_ref[p, head:, :rows] = zeros
            pairs_ref[p, head:, rows:] = odd
        stat[:HEADS] = jnp.full((HEADS, rows), NEG_FILL, F32)
        stat[HEADS:] = jnp.zeros((HEADS, rows), F32)
        acc[...] = jnp.zeros(acc.shape, F32)
    else:
        acc[...] = acc_in[...]
        stat[...] = stat_in[...]
    scale = head ** (-0.5) * LOG2E

    def one_tile(t, carry):
        @pl.when(here_served(slot_of(t)))
        def _():
            fetch(next(iter(served)), t).wait()
            scores = []
            for p in range(HEADS // 2):
                keys = tile_vmem[t, :, 2 * p * head : (2 * p + 2) * head]
                scores.append(dot(keys, pairs_ref[p]))
            vals = tile_vmem[t, :, width:].T
            for p in range(HEADS // 2):
                old = jnp.concatenate([stat[2 * p : 2 * p + 1], stat[2 * p + 1 : 2 * p + 2]], axis=1)
                new = jnp.maximum(old, jnp.max(scores[p], axis=0, keepdims=True))
                alpha = jnp.exp2((old - new) * scale)
                w = jnp.exp2((scores[p] - new) * scale)
                total = jnp.sum(w, axis=0, keepdims=True)
                w = w.astype(BF16)
                for side in range(2):
                    h = 2 * p + side
                    half = slice(side * rows, (side + 1) * rows)
                    mine = slice(h * head, (h + 1) * head)
                    stat[h : h + 1] = new[:, half]
                    stat[HEADS + h : HEADS + h + 1] = stat[HEADS + h : HEADS + h + 1] * alpha[:, half] + total[:, half]
                    acc[mine, :] = acc[mine, :] * alpha[:, half] + dot(vals[mine, :], w[:, half])

        return carry

    lax.fori_loop(0, n_tiles, one_tile, 0)
    if last:
        acc_out[...] = acc[...].T
        pad = jnp.zeros((LANES - 2 * HEADS, rows), F32)
        stat_out[...] = jnp.concatenate([stat[...], pad], axis=0).T


def rows_in_order(refs, j, bucket, first, width):
    parts = []
    for ref in refs:
        top = ref.shape[0] - (MATCHINGS - j) * bucket
        left = first if ref.shape[1] == 2 * width else 0
        parts.append(ref[top : top + bucket, left : left + width])
    return jnp.concatenate(parts, axis=0)


def score_kernel(groups, q_ref, order_ref, bias_ref, *refs):
    key_refs = refs[:groups]
    score_ref = refs[groups]
    rows, width = q_ref.shape
    head = width // HEADS
    bucket = rows // groups
    gather = (
        lax.broadcasted_iota(jnp.int32, (width, LANES), 0) // head
        == lax.broadcasted_iota(jnp.int32, (width, LANES), 1)
    )
    gather = jnp.where(gather, 1.0, 0.0).astype(BF16)
    queries = q_ref[...].astype(F32)
    for j in range(MATCHINGS):
        table = place_table(order_ref[j : j + 1, :], rows)
        prod = queries * dot(table, rows_in_order(key_refs, j, bucket, 0, width))
        high = prod.astype(BF16)
        low = (prod - high.astype(F32)).astype(BF16)
        score_ref[j] = dot(high, gather) + dot(low, gather) + bias_ref[j : j + 1, :] * head**0.5


def weigh_kernel(groups, order_ref, acc_ref, stat_ref, score_ref, *refs):
    val_refs = refs[: groups - 1]
    part_ref, edge_ref = refs[groups - 1 :]
    rows, width = part_ref.shape
    head = width // HEADS
    bucket = rows // groups
    scale = head ** (-0.5) * LOG2E
    spread = (
        lax.broadcasted_iota(jnp.int32, (LANES, width), 1) // head
        == lax.broadcasted_iota(jnp.int32, (LANES, width), 0)
    )
    spread = jnp.where(spread, 1.0, 0.0).astype(BF16)
    stat = stat_ref[...]
    lane = lax.broadcasted_iota(jnp.int32, stat.shape, 1)
    block_max = jnp.where(lane < HEADS, stat, 0.0)
    block_sum = jnp.where(lane < HEADS, jnp.roll(stat, -HEADS, axis=1), 1.0)
    edge_scores = [score_ref[j] for j in range(MATCHINGS)]
    top = block_max
    for edge in edge_scores:
        top = jnp.maximum(top, edge)
    keep = jnp.exp2((block_max - top) * scale)
    edge_w = [jnp.exp2((edge - top) * scale) for edge in edge_scores]
    total = block_sum * keep
    for u in edge_w:
        total = total + u
    inv = 1.0 / total

    def wide(x):
        high = x.astype(BF16)
        low = (x - high.astype(F32)).astype(BF16)
        return dot(high, spread) + dot(low, spread)

    numer = acc_ref[...] * wide(keep * inv)
    for j in range(MATCHINGS):
        table = place_table(order_ref[j : j + 1, :], rows)
        share = edge_w[j].astype(BF16).astype(F32) * inv
        numer = numer + wide(share) * dot(table[:, : rows - bucket], rows_in_order(val_refs, j, bucket, width, width))
        high = share.astype(BF16)
        low = (share - high.astype(F32)).astype(BF16)
        last = table[:, rows - bucket :]
        in_order = dot(last, high, ((0,), (0,))) + dot(last, low, ((0,), (0,)))
        edge_ref[j * bucket : (j + 1) * bucket, :] = wide(in_order)
    part_ref[...] = numer


def finish_kernel(groups, val_ref, order_ref, part_ref, edge_ref, w_ref, out_ref):
    rows, width = part_ref.shape
    bucket = rows // groups
    weighed = edge_ref[...] * val_ref[:, val_ref.shape[1] - width :].astype(F32)
    high = weighed.astype(BF16)
    low = (weighed - high.astype(F32)).astype(BF16)
    tables = [place_table(order_ref[j : j + 1, :], rows)[:, rows - bucket :] for j in range(MATCHINGS)]
    table = jnp.concatenate(tables + tables, axis=1)
    attended = part_ref[...] + dot(table, jnp.concatenate([high, low], axis=0))
    out_ref[...] = dot(attended.astype(BF16), w_ref[...]).astype(BF16)


fence = lax.optimization_barrier


def vmem_specs(n):
    return [pl.BlockSpec(memory_space=pltpu.VMEM)] * n


def shards(groups, loop_size, queries, key_rows, value_rows, out_weight, tile_list, expander_order, expander_bias):
    rows, width = queries.shape
    head = width // HEADS
    bucket = rows // groups
    params = pltpu.CompilerParams(vmem_limit_bytes=VMEM_BYTES)
    tile_shape = jax.ShapeDtypeStruct((rows, 2 * width), BF16)
    relayed = loop_size == 8 and groups == 4
    kv_shape = jax.ShapeDtypeStruct((MATCHINGS * bucket, 2 * width), BF16)
    one_shape = jax.ShapeDtypeStruct((MATCHINGS * bucket, width), BF16)
    full_shape = jax.ShapeDtypeStruct((rows + ORDER_ROWS, width), BF16)
    bucket_shapes = [kv_shape, full_shape] if relayed else [kv_shape] * groups
    own_tile, *outgoing = pl.pallas_call(
        functools.partial(prep_kernel, groups, 1 if relayed else 0),
        out_shape=[tile_shape] + bucket_shapes,
        in_specs=[pl.BlockSpec(memory_space=pltpu.HBM)] * 3,
        out_specs=vmem_specs(1 + len(bucket_shapes)),
        scratch_shapes=[
            pltpu.VMEM(expander_order.shape, jnp.int32),
            pltpu.SemaphoreType.DMA((3,)),
        ],
        compiler_params=params,
        name="prep",
    )(*[pltpu.with_memory_space_constraint(x, pltpu.HBM) for x in (key_rows, value_rows, expander_order)])

    def over_grp(array, b):
        return lax.ppermute(array, "grp", [(i, i ^ b) for i in range(groups)])

    def flipped(array, bits):
        return lax.ppermute(array, "loop", [(i, i ^ bits) for i in range(loop_size)])

    def attend(served, state, last):
        shapes = [(width, rows), (2 * HEADS, rows)]
        if last:
            shapes = [(rows, width), (rows, LANES)] + shapes
        out_shape = [jax.ShapeDtypeStruct(shape, F32) for shape in shapes[:2]]
        scratch = [pltpu.VMEM(shape, F32) for shape in shapes[2:]]
        pairs_shape = jax.ShapeDtypeStruct((HEADS // 2, 2 * head, 2 * rows), BF16)
        if state is None:
            out_shape.append(pairs_shape)
        others = [queries] if state is None else state
        aliases = {} if state is None or last else {len(served) + 2: 0, len(served) + 3: 1}
        acc, stat, *pairs = pl.pallas_call(
            functools.partial(blocks_kernel, loop_size, tuple(served), state is None, last),
            out_shape=out_shape,
            in_specs=[pl.BlockSpec(memory_space=pltpu.SMEM)]
            + [pl.BlockSpec(memory_space=pl.ANY)] * len(served)
            + vmem_specs(len(others)),
            out_specs=vmem_specs(len(out_shape)),
            scratch_shapes=scratch
            + [
                pltpu.VMEM((tile_list.shape[1],) + tile_shape.shape, BF16),
                pltpu.SemaphoreType.DMA((tile_list.shape[1],)),
            ],
            input_output_aliases=aliases,
            compiler_params=params,
            cost_estimate=pl.CostEstimate(flops=1000, bytes_accessed=1000, transcendentals=0) if state is None else CHEAP,
            name="blocks" + "_".join(map(str, served)),
        )(tile_list, *served.values(), *others)
        return [pairs[0] if state is None else state[0], acc, stat]

    bias = jnp.pad(expander_bias, ((0, 0), (0, LANES - HEADS)))

    def score(key_parts):
        return pl.pallas_call(
            functools.partial(score_kernel, groups),
            out_shape=jax.ShapeDtypeStruct((MATCHINGS, rows, LANES), F32),
            in_specs=vmem_specs(3 + groups),
            out_specs=pl.BlockSpec(memory_space=pltpu.VMEM),
            compiler_params=params,
            cost_estimate=CHEAP,
            name="score",
        )(queries, expander_order, bias, *key_parts)

    if relayed:

        def relay(order, full, name):
            return pl.pallas_call(
                functools.partial(relay_kernel, groups),
                out_shape=[one_shape] * 2,
                in_specs=vmem_specs(2),
                out_specs=vmem_specs(2),
                compiler_params=params,
                cost_estimate=pl.CostEstimate(flops=10**10 if name == "relay_keys" else 2*10**9, bytes_accessed=1000, transcendentals=0),
                name=name,
            )(order, full)

        full_k = over_grp(outgoing[1], 2)
        near = over_grp(outgoing[0], 1)
        across = flipped(own_tile, 5)
        side = flipped(own_tile, 2)
        twin = flipped(own_tile, 1)
        state = attend({0: own_tile}, None, False)
        full_k, own_vals, state = fence((full_k, value_rows, state))
        full_v = over_grp(own_vals, 2)
        keys_2, passed = relay(full_k, full_k, "relay_keys")
        across, side, twin, state, keys_2, passed = fence((across, side, twin, state, keys_2, passed))
        corner_twin = flipped(across, 2)
        corner = flipped(side, 4)
        side_twin = flipped(side, 1)
        keys_3 = over_grp(passed, 1)
        state = attend({1: twin, 2: side, 4: across}, state, False)
        own_bucket = pl.pallas_call(
            functools.partial(own_bucket_kernel, groups),
            out_shape=kv_shape,
            in_specs=vmem_specs(2),
            out_specs=pl.BlockSpec(memory_space=pltpu.VMEM),
            compiler_params=params,
            cost_estimate=CHEAP,
            name="own_bucket",
        )(own_tile, expander_order)
        full_v, near, state, own_bucket = fence((full_v, near, state, own_bucket))
        state = attend({3: side_twin}, state, False)
        vals_2, passed = relay(full_k, full_v, "relay_vals")
        vals_3 = over_grp(passed, 1)
        val_parts = [own_bucket, near, vals_2, vals_3]
        late = {5: corner, 6: corner_twin}
        _, acc, stat = attend(late, state, True)
        keys_3, acc, stat = fence((keys_3, acc, stat))
        scores = score([own_bucket, near, keys_2, keys_3])
    else:
        tiles = {}
        for offset in range(-RADIUS, RADIUS + 1):
            pairs = [(i, (i - offset) % loop_size) for i in range(loop_size)]
            tile = lax.ppermute(own_tile, "loop", pairs) if offset else own_tile
            tiles[offset + RADIUS] = tile
        _, acc, stat = attend(tiles, None, True)
        val_parts = [outgoing[0]] + [over_grp(outgoing[b], b) for b in range(1, groups)]
        scores = score(val_parts)

    part, edge = pl.pallas_call(
        functools.partial(weigh_kernel, groups),
        out_shape=[
            jax.ShapeDtypeStruct((rows, width), F32),
            jax.ShapeDtypeStruct((MATCHINGS * bucket, width), F32),
        ],
        in_specs=vmem_specs(3 + groups),
        out_specs=vmem_specs(2),
        compiler_params=params,
        cost_estimate=CHEAP,
        name="weigh",
    )(expander_order, acc, stat, scores, *val_parts[:-1])
    return pl.pallas_call(
        functools.partial(finish_kernel, groups),
        out_shape=jax.ShapeDtypeStruct((rows, width), BF16),
        in_specs=vmem_specs(5),
        out_specs=pl.BlockSpec(memory_space=pltpu.VMEM),
        compiler_params=params,
        cost_estimate=CHEAP,
        name="finish",
    )(val_parts[-1], expander_order, part, edge, out_weight)


def solution(mesh):
    placed = (
        P(("loop", "grp"), None),
        P(("loop", "grp"), None),
        P(("loop", "grp"), None),
        P(),
        P(("loop", "grp"), None),
        P(None, ("loop", "grp")),
        P(),
    )
    return jax.shard_map(
        functools.partial(shards, mesh.shape["grp"], mesh.shape["loop"]),
        mesh=mesh,
        in_specs=placed,
        out_specs=P(("loop", "grp"), None),
        check_vma=False,
    )
```
